256 devices in a mesh: space: 32 (over y, z_hi, core), tm: 8 (over z_lo, x).
Axes of the slice: x: 4, y: 4, z: 8 (z_hi: 4, z_lo: 2; z = z_hi * 2 + z_lo), core: 2. Of those that a mesh axis runs over, the one named last changes fastest.
Arguments:
- activity: bfloat16 [2048, 256, 512], P('space', 'tm'), may hold values from 0 to 8
- footprints: bfloat16 [32, 8, 16, 4, 512], P('space'), may hold values from 0.0099487305 to 1
- traces: float32 [32, 8, 16, 256], P('space', None, None, 'tm'), may hold values from 0.1 to 2
- bg_space: float32 [2, 2048, 512], P(None, 'space'), may hold values from 0.05 to 14, as said below
- bg_time: float32 [2, 256], P(None, 'tm'), may hold values from 0.5 to 2
- block_lists: int32 [32, 8, 4], P('space'), may hold values from 0 to 71, as said below
- group_order: int32 [32, 8], P('space'), may hold values from 0 to 7, each once within a row
Outputs:
- traces_out: float32 [32, 8, 16, 256], P('space', None, None, 'tm')
- footprints_out: bfloat16 [32, 8, 16, 4, 512], P('space')
- bg_space_out: float32 [2, 2048, 512], P(None, 'space')
- bg_time_out: float32 [2, 256], P(None, 'tm')
The draws below stay inside these ranges and needn't reach their ends.
Inputs may be any that keep to these rules, and one draw needn't show every extreme that they name: `block_lists`: the 4 entries of a group differ. Entries below 4 or from 68 on lie in a neighbouring tile; a group has at most one of them, never one outside the grid, and each such entry of a tile with both neighbours is held by exactly one of its groups. `group_order`: each tile's row holds every group number once. `bg_space`: Positive.
All inputs are finite; a program needn't handle non-finite values.
Results may differ from the reference program's by a relative error of at most 0.014.
The reference program's roundings to bfloat16 on the way count: a program that leaves them out, or rounds other values in their place, can miss the bound.
Values may be sent and summed in bfloat16 or wider, within the bound.
A program may use at most 128 MiB of HBM per device.

```python
import math
import jax
import jax.numpy as jnp
from jax import lax

G = 16
NG_DEV = 8
BPG = 4
BV = 512
VB = 64
ROUNDS = 2
HB = 4
TILES = 32
NBLK = 2048
FRAMES = 256


def draw_block_lists(key, part):
    key = jax.random.fold_in(key, 7)
    core_keys = jax.random.split(jax.random.fold_in(key, 1), TILES * NG_DEV)
    core_blocks = jax.vmap(lambda k: jax.random.permutation(k, VB)[:BPG])(core_keys)
    core_blocks = core_blocks.reshape(TILES, NG_DEV, BPG).astype(jnp.int32) + HB
    side_keys = jax.random.split(jax.random.fold_in(key, 2), TILES)
    slot_rank = jax.vmap(lambda k: jax.random.permutation(k, NG_DEV))(side_keys).astype(jnp.int32)
    tile_ids = jnp.arange(TILES, dtype=jnp.int32)[:, None]
    halo_block = jnp.where(slot_rank < HB, slot_rank, VB + slot_rank)
    usable = jnp.where(slot_rank < HB, tile_ids > 0, tile_ids < TILES - 1)
    leading = jnp.where(usable, halo_block, core_blocks[:, :, 0])
    return jnp.concatenate([leading[:, :, None], core_blocks[:, :, 1:]], 2).astype(jnp.int32)


def draw_bg_space(key, part):
    key = jax.random.fold_in(key, 5)
    position = jnp.arange(NBLK * BV, dtype=jnp.float32).reshape(NBLK, BV) / (NBLK * BV)
    rising = 1.0 + 2.0 * position
    values = jnp.exp(jax.random.uniform(key, (2, NBLK, BV), jnp.float32, math.log(0.1), math.log(0.6)))
    return values * rising[None]


def block_levels(key, dims, cuts, least, top_value):
    def one(dim, blocks):
        steps = jax.random.uniform(jax.random.fold_in(jax.random.fold_in(key, 6), dim), (blocks,), jnp.float32, least / len(cuts), top_value / len(cuts))
        return jnp.repeat(jnp.exp(steps), dims[dim] // blocks).reshape((-1,) + (1,) * (len(dims) - dim - 1))

    loudness = one(*cuts[0])
    for cut in cuts[1:]:
        loudness = loudness * one(*cut)
    return loudness


def setup_inputs(seed: int = 0) -> dict:
    streams_of = jax.random.split(jax.random.key(seed), 8)
    return {
        "activity": jnp.clip(8.0 * jax.random.uniform(streams_of[0], (NBLK, FRAMES, BV), jnp.float32) ** block_levels(streams_of[0], (NBLK, FRAMES, BV), ((0, 32), (1, 8)), -0.2, 0.2), 0.0, 8.0).astype(jnp.bfloat16),
        "footprints": jnp.clip(jnp.exp(math.log(1.0) - 4.61031033 * jax.random.uniform(streams_of[1], (TILES, NG_DEV, G, BPG, BV), jnp.float32) ** block_levels(streams_of[1], (TILES, NG_DEV, G, BPG, BV), ((0, 32),), -0.2, 0.2)), 0.0099487305, 1.0).astype(jnp.bfloat16),
        "traces": jnp.clip(jnp.exp(math.log(2.0) - 2.9957323 * jax.random.uniform(streams_of[2], (TILES, NG_DEV, G, FRAMES), jnp.float32) ** block_levels(streams_of[2], (TILES, NG_DEV, G, FRAMES), ((0, 32), (3, 8)), -0.2, 0.2)), 0.1, 2.0),
        "bg_space": draw_bg_space(jax.random.fold_in(streams_of[7], 71), 0),
        "bg_time": jnp.clip(jnp.exp(math.log(2.0) - 1.3862944 * jax.random.uniform(streams_of[4], (2, FRAMES), jnp.float32) ** block_levels(streams_of[4], (2, FRAMES), ((1, 8),), -0.2, 0.2)), 0.5, 2.0),
        "block_lists": draw_block_lists(jax.random.fold_in(streams_of[7], 71), 0),
        "group_order": jax.vmap(lambda own: jax.random.permutation(own, NG_DEV))(jax.random.split(streams_of[6], TILES)).reshape((TILES, NG_DEV)).astype(jnp.int32),
    }


ridge_trace = 0.01
ridge_foot = 0.1

def group_inverse(matrices):
    lower_factor = jnp.linalg.cholesky(matrices)
    identity = jnp.broadcast_to(jnp.eye(matrices.shape[-1], dtype=matrices.dtype), matrices.shape)
    inverse_low = lax.linalg.triangular_solve(lower_factor, identity, left_side=True, lower=True)
    return jnp.einsum('gji,gjk->gik', inverse_low, inverse_low, precision=lax.Precision.HIGHEST)

def tile_gram(footprint, block_row):
    flattened = footprint.reshape(-1, footprint.shape[-1])
    paired = jnp.dot(flattened.astype(jnp.float32), flattened.T.astype(jnp.float32), preferred_element_type=jnp.float32)
    groups, members, extent = (footprint.shape[0], footprint.shape[1], footprint.shape[2])
    paired = paired.reshape(groups, members, extent, groups, members, extent)
    shared = (block_row[:, :, None, None] == block_row[None, None, :, :]).astype(jnp.float32)
    return jnp.sum(paired * shared[:, None, :, :, None, :], axis=(2, 5))

def tile_rebuild(footprint, trace_low, block_row):
    contrib = jnp.einsum('gnkv,gnt->gktv', footprint.astype(jnp.float32), trace_low.astype(jnp.float32))
    shaped = contrib.reshape(-1, contrib.shape[2], contrib.shape[3])
    empty_ext = jnp.zeros((VB + 2 * HB, shaped.shape[1], shaped.shape[2]), jnp.float32)
    return empty_ext.at[block_row.reshape(-1)].add(shaped)

def residual_all(activity, footprints, trace_low, bg_space, bg_time, block_lists):
    tile_ids = jnp.arange(TILES, dtype=jnp.int32)

    def spills(tile_id):
        rebuilt = tile_rebuild(footprints[tile_id], trace_low[tile_id], block_lists[tile_id])
        return (rebuilt[:HB], rebuilt[HB + VB:])
    left_spill, right_spill = lax.map(spills, tile_ids)
    zero_spill = jnp.zeros_like(right_spill[:1])
    from_left = jnp.concatenate([zero_spill, right_spill[:-1]], 0)
    from_right = jnp.concatenate([left_spill[1:], zero_spill], 0)

    def central(tile_id):
        rebuilt = tile_rebuild(footprints[tile_id], trace_low[tile_id], block_lists[tile_id])
        middle = rebuilt[HB:HB + VB]
        middle = middle.at[:HB].add(from_left[tile_id]).at[VB - HB:].add(from_right[tile_id])
        observed = lax.dynamic_slice_in_dim(activity, tile_id * VB, VB, 0).astype(jnp.float32)
        spatial = lax.dynamic_slice_in_dim(bg_space, tile_id * VB, VB, 1)
        backdrop = jnp.einsum('cbv,ct->btv', spatial, bg_time, precision=lax.Precision.HIGHEST)
        return (observed - middle - backdrop).astype(jnp.bfloat16)
    return lax.map(central, tile_ids)

def extended(residue, tile_id):
    before = residue[jnp.maximum(tile_id - 1, 0)][VB - HB:]
    following = residue[jnp.minimum(tile_id + 1, TILES - 1)][:HB]
    before = jnp.where(tile_id > 0, before, jnp.zeros_like(before))
    following = jnp.where(tile_id < TILES - 1, following, jnp.zeros_like(following))
    return jnp.concatenate([before, residue[tile_id], following], 0)

def pieces_of(extended_res, block_row):
    return extended_res[block_row.reshape(-1)].reshape(NG_DEV, BPG, extended_res.shape[1], BV)

def temporal(tile_id, residue, footprints, traces, block_lists, group_order):
    footprint = footprints[tile_id]
    block_row = block_lists[tile_id]
    pieces = pieces_of(extended(residue, tile_id), block_row)
    drives = jnp.einsum('gnkv,gktv->gnt', footprint.astype(jnp.float32), pieces.astype(jnp.float32))
    gram_matrix = tile_gram(footprint, block_row)
    members = footprint.shape[1]
    picks = jnp.arange(NG_DEV)
    diagonal = gram_matrix[picks, :, picks, :]
    inverse = group_inverse(diagonal + ridge_trace * BPG * BV * jnp.eye(members, dtype=jnp.float32))
    started = traces[tile_id]
    current = started
    for position in range(NG_DEV):
        chosen = group_order[tile_id, position]
        coupling = gram_matrix[chosen].reshape(members, -1)
        change = (current - started).reshape(-1, current.shape[-1])
        remain = drives[chosen] - jnp.dot(coupling, change, precision=lax.Precision.HIGHEST)
        updated = jnp.maximum(current[chosen] + jnp.dot(inverse[chosen], remain, precision=lax.Precision.HIGHEST), 0.0)
        current = current.at[chosen].set(updated)
    return current

def spatial_tile(tile_id, residue, footprints, trace_mid, trace_low, bg_space, bg_time, block_lists):
    observed = residue[tile_id].astype(jnp.float32)
    spatial = lax.dynamic_slice_in_dim(bg_space, tile_id * VB, VB, 1)
    voxel_part = jnp.einsum('cbv,btv->ct', spatial, observed, precision=lax.Precision.HIGHEST)
    frame_part = jnp.einsum('btv,ct->cbv', observed, bg_time, precision=lax.Precision.HIGHEST)
    pieces = pieces_of(extended(residue, tile_id), block_lists[tile_id])
    current = trace_mid[tile_id]
    low_current = lax.optimization_barrier(trace_low[tile_id]).astype(jnp.float32)
    project = jnp.einsum('gnt,gktv->gnkv', low_current, pieces.astype(jnp.float32))
    correlation = jnp.einsum('gnt,gmt->gnm', current, current, precision=lax.Precision.HIGHEST)
    eye_small = jnp.eye(current.shape[1], dtype=jnp.float32)
    inverse = group_inverse(correlation + ridge_foot * FRAMES * eye_small)
    moved = jnp.einsum('gnm,gmkv->gnkv', inverse, project, precision=lax.Precision.HIGHEST)
    renewed = jnp.maximum(footprints[tile_id].astype(jnp.float32) + moved, 0.0).astype(jnp.bfloat16)
    return (renewed, voxel_part, frame_part)

def reference(activity, footprints, traces, bg_space, bg_time, block_lists, group_order):
    tile_ids = jnp.arange(TILES, dtype=jnp.int32)
    for round_id in range(ROUNDS):
        trace_low = traces.astype(jnp.bfloat16)
        residue = residual_all(activity, footprints, trace_low, bg_space, bg_time, block_lists)
        traces = lax.map(lambda tile_id: temporal(tile_id, residue, footprints, traces, block_lists, group_order), tile_ids)
        trace_low = traces.astype(jnp.bfloat16)
        residue = residual_all(activity, footprints, trace_low, bg_space, bg_time, block_lists)
        renewed, voxel_parts, frame_parts = lax.map(lambda tile_id: spatial_tile(tile_id, residue, footprints, traces, trace_low, bg_space, bg_time, block_lists), tile_ids)
        voxel_sum = jnp.sum(voxel_parts, 0)
        frame_sum = jnp.transpose(frame_parts, (1, 0, 2, 3)).reshape(2, TILES * VB, BV)
        squares_space = jnp.sum(bg_space * bg_space, axis=(1, 2))
        squares_time = jnp.sum(bg_time * bg_time, axis=1)
        new_time = jnp.maximum(bg_time + voxel_sum / (2.0 * squares_space[:, None]), 0.0)
        bg_space = jnp.maximum(bg_space + frame_sum / (2.0 * squares_time[:, None, None]), 0.0)
        bg_time = new_time
        footprints = renewed
    return (traces, footprints, bg_space, bg_time)
```

```python
import functools

import jax
import jax.numpy as jnp
from jax import lax
from jax.experimental import pallas as pl
from jax.experimental.pallas import tpu as pltpu
from jax.sharding import PartitionSpec as P

MESH = pl.DeviceIdType.MESH
HIGH = lax.Precision.HIGHEST
F32 = jnp.float32
BF16 = jnp.bfloat16

G = 16
NG = 8
NC = NG * G
BPG = 4
BV = 512
VB = 64
EXT = 72
FR = 32
NT = 8
ROUNDS = 2
RIDGE_TRACE = 0.01 * BPG * BV
RIDGE_FOOT = 0.1 * FR * NT


def dot(a, b, precision=None):
    return lax.dot_general(a, b, (((1,), (0,)), ((), ())), precision=precision, preferred_element_type=F32)


def dot_nt(a, b, precision=None):
    return lax.dot_general(a, b, (((1,), (1,)), ((), ())), precision=precision, preferred_element_type=F32)


def split3(x):
    hi = x.astype(BF16).astype(F32)
    rest = x - hi
    mid = rest.astype(BF16).astype(F32)
    return hi, mid, rest - mid


def lanes(rows):
    return lax.broadcasted_iota(jnp.int32, (rows, NC), 1)


def fold_diagonal(square):
    group = lanes(G) // G
    out = jnp.zeros((G, NC), F32)
    for h in range(NG):
        out = out + jnp.where(group == h, square[h * G : (h + 1) * G], 0.0)
    return out


def spread_diagonal(folded):
    group = lanes(G) // G
    return jnp.concatenate([jnp.where(group == h, folded, 0.0) for h in range(NG)], axis=0)


def inverse_blocks(folded, ridge):
    first = lanes(G) % G
    sub = lax.broadcasted_iota(jnp.int32, (G, NC), 0)
    folded = folded + jnp.where(sub == first, ridge, 0.0)
    rows = []
    for n in range(G):
        moved = folded if n == 0 else pltpu.roll(folded, NC - n, 1)
        rows.append(jnp.where(first == 0, moved, jnp.where(sub == n, 1.0, 0.0)))
    for p in range(G):
        pivot = 1.0 / rows[p][p : p + 1]
        at = sub == p
        scaled = jnp.where(at, jnp.broadcast_to(pivot, (G, NC)), rows[p] * pivot)
        for n in range(G):
            if n != p:
                rows[n] = jnp.where(at, 0.0, rows[n]) - rows[n][p : p + 1] * scaled
        rows[p] = scaled
    out = jnp.zeros((G, NC), F32)
    for n in range(G):
        moved = rows[n] if n == 0 else pltpu.roll(rows[n], n, 1)
        out = jnp.where(first == n, moved, out)
    return spread_diagonal(out)


def kernel(
    nsp, levels,
    act, f0, tr0, bg0, bt0, bl, order,
    out_tr, out_f, out_bg, out_bt,
    blrow, res, pieces, foot, bgs, bts, halo_f, halo_out, tl_in, tl_out, corr_out, corr_in, sb, rb, vacc, vox, bgn, zs, btm,
    nb_s, nb_r, tm_s, tm_r, vx_s, vx_r,
):
    me = lax.axis_index("tm")
    sp = lax.axis_index("space")
    left = lax.rem(sp + nsp - 1, nsp)
    right = lax.rem(sp + 1, nsp)
    peers = []
    for stride, size in levels:
        q = lax.rem(sp // stride, size)
        row = []
        for d in range(1, size):
            other = lax.rem(q + d, size)
            row.append((sp + (other - q) * stride, other))
        peers.append((q, row))

    barrier = pltpu.get_barrier_semaphore()
    count = 0
    for d in range(1, NT):
        pl.semaphore_signal(barrier, inc=1, device_id=(sp, lax.rem(me + d, NT)), device_id_type=MESH)
        count += 1
    for other in (left, right):
        pl.semaphore_signal(barrier, inc=1, device_id=(other, me), device_id_type=MESH)
        count += 1
    for _, row in peers:
        for other, _ in row:
            pl.semaphore_signal(barrier, inc=1, device_id=(other, me), device_id_type=MESH)
            count += 1

    sends = []

    def send(src, dst, ssem, rsem, device):
        copy = pltpu.make_async_remote_copy(
            src_ref=src, dst_ref=dst, send_sem=ssem, recv_sem=rsem, device_id=device, device_id_type=MESH
        )
        copy.start()
        sends.append(copy)

    def arrived(ref, ssem, rsem, device):
        pltpu.make_async_remote_copy(
            src_ref=ref, dst_ref=ref, send_sem=ssem, recv_sem=rsem, device_id=device, device_id_type=MESH
        ).wait_recv()

    def to_neighbours(cat, src_left, src_right, dst):
        send(src_right, dst(0), nb_s.at[cat, 0], nb_r.at[cat, 0], (right, me))
        send(src_left, dst(1), nb_s.at[cat, 1], nb_r.at[cat, 1], (left, me))

    def from_neighbours(cat, dst):
        arrived(dst(0), nb_s.at[cat, 0], nb_r.at[cat, 0], (left, me))
        arrived(dst(1), nb_s.at[cat, 1], nb_r.at[cat, 1], (right, me))

    entry = [[bl[g, k] for k in range(BPG)] for g in range(NG)]
    group32 = lanes(FR) // G

    for k in range(BPG):
        row = jnp.zeros((FR, NC), jnp.int32)
        for g in range(NG):
            row = jnp.where(group32 == g, entry[g][k], row)
        blrow[:, k * NC : (k + 1) * NC] = row
    halo_id = jnp.full((G, NC), -1, jnp.int32)
    halo_k = []
    group16 = lanes(G) // G
    for g in range(NG):
        hid = jnp.int32(-1)
        hk = jnp.int32(0)
        for k in range(BPG):
            out = jnp.logical_or(entry[g][k] < 4, entry[g][k] >= 68)
            hid = jnp.where(out, entry[g][k], hid)
            hk = jnp.where(out, k, hk)
        halo_id = jnp.where(group16 == g, hid, halo_id)
        halo_k.append(hk)
    halo_bf = halo_id.astype(F32).astype(BF16)

    def stage_halo(r, source):
        for g in range(NG):
            halo_out[r, g * G : (g + 1) * G, :] = source[halo_k[g], g * G : (g + 1) * G, :]

    def stage_traces(i, low):
        tl_out[i, 0:FR, :] = low
        tl_out[i, FR : FR + G, :] = halo_bf

    def gram_of(source):
        everything = source[...].reshape(BPG * NC, BV)
        total = jnp.zeros((NC, NC), F32)
        for k in range(BPG):
            product = dot_nt(source[k], everything)
            column = jnp.concatenate([jnp.full((G, NC), entry[g][k], jnp.int32) for g in range(NG)], axis=0)
            for j in range(BPG):
                row = blrow[:, j * NC : (j + 1) * NC]
                row = jnp.concatenate([row] * (NC // FR), axis=0)
                total = total + jnp.where(column == row, product[:, j * NC : (j + 1) * NC], 0.0)
        return total

    def chunk(inst, j, source, space, low4, traces_i, r, side, with_bg):
        parts = []
        for i in range(8):
            parts.append(jnp.where(blrow[...] == 8 * j + 4 + i, low4, 0.0).astype(BF16))
        lhs = jnp.concatenate(parts, axis=0)
        rebuilt = dot(lhs, source[...].reshape(BPG * NC, BV))
        if side is not None:
            low = tl_in[traces_i, side, 0:FR, :].astype(F32)
            hid = tl_in[traces_i, side, FR : FR + G, :].astype(F32)
            hid = jnp.concatenate([hid, hid], axis=0)
            base = 68.0 if side == 0 else 0.0
            near = jnp.concatenate(
                [jnp.where(hid == base + i, low, 0.0).astype(BF16) for i in range(4)], axis=0
            )
            near = dot(near, halo_f[r, side])
            if side == 0:
                rebuilt = jnp.concatenate([rebuilt[: 4 * FR] + near, rebuilt[4 * FR :]], axis=0)
            else:
                rebuilt = jnp.concatenate([rebuilt[: 4 * FR], rebuilt[4 * FR :] + near], axis=0)
        t0 = jnp.concatenate([bts[0]] * (BV // NC), axis=1)
        t1 = jnp.concatenate([bts[1]] * (BV // NC), axis=1)
        s0 = space[0, pl.ds(8 * j, 8), :]
        s1 = space[1, pl.ds(8 * j, 8), :]
        out = []
        for i in range(8):
            backdrop = s0[i : i + 1] * t0 + s1[i : i + 1] * t1
            seen = act[8 * j + i].astype(F32)
            value = ((seen - rebuilt[i * FR : (i + 1) * FR]) - backdrop).astype(BF16)
            res[inst, 8 * j + 4 + i] = value
            out.append(value)
        if with_bg:
            flat = jnp.concatenate(out, axis=0)
            frame = dot(btm[...], flat)
            sb[r, j, 64:80, :] = (frame[0:16] + frame[16:32] + frame[32:48]).astype(BF16)
            s = jnp.concatenate([s0, s1], axis=0)
            s = jnp.concatenate([x.astype(BF16) for x in split3(s)], axis=0)
            vacc[...] += dot_nt(flat, s)

    def residual(inst, source, space, low, traces_i, r, with_bg):
        low4 = jnp.concatenate([low.astype(F32)] * BPG, axis=1)
        chunk(inst, 0, source, space, low4, traces_i, r, 0, with_bg)
        chunk(inst, 7, source, space, low4, traces_i, r, 1, with_bg)
        cat = 5 + inst
        send(res.at[inst, pl.ds(64, 4)], res.at[inst, pl.ds(0, 4)], nb_s.at[cat, 0], nb_r.at[cat, 0], (right, me))
        send(res.at[inst, pl.ds(4, 4)], res.at[inst, pl.ds(68, 4)], nb_s.at[cat, 1], nb_r.at[cat, 1], (left, me))

        def body(j, carry):
            chunk(inst, j, source, space, low4, traces_i, r, None, with_bg)
            return carry

        lax.fori_loop(1, 7, body, 0)

    def gather(inst):
        cat = 5 + inst
        arrived(res.at[inst, pl.ds(0, 4)], nb_s.at[cat, 0], nb_r.at[cat, 0], (left, me))
        arrived(res.at[inst, pl.ds(68, 4)], nb_s.at[cat, 1], nb_r.at[cat, 1], (right, me))
        for g in range(NG):
            for k in range(BPG):
                pieces[k, g * FR : (g + 1) * FR, :] = res[inst, entry[g][k]]

    traces_now = tr0[...]
    bts[...] = bt0[...]
    low = traces_now.astype(BF16)
    stage_halo(0, f0)
    stage_traces(0, low)

    pl.semaphore_wait(barrier, count)
    to_neighbours(0, halo_out.at[0], halo_out.at[0], lambda s: halo_f.at[0, s])
    to_neighbours(2, tl_out.at[0], tl_out.at[0], lambda s: tl_in.at[0, s])

    for r in range(ROUNDS):
        source = f0 if r == 0 else foot.at[0]
        space = bg0 if r == 0 else bgs.at[0]
        gram = gram_of(source)
        inverse = inverse_blocks(fold_diagonal(gram), RIDGE_TRACE)
        weights = dot(gram, inverse, HIGH)

        from_neighbours(r, lambda s: halo_f.at[r, s])
        if r == 0:
            from_neighbours(2, lambda s: tl_in.at[0, s])
        residual(2 * r, source, space, low, r, r, False)
        gather(2 * r)
        cross = jnp.zeros((NG * FR, NC), F32)
        for k in range(BPG):
            cross = cross + dot_nt(pieces[k], source[k])
        drives = jnp.zeros((FR, NC), F32)
        for g in range(NG):
            drives = drives + jnp.where(group32 == g, cross[g * FR : (g + 1) * FR], 0.0)
        drives = dot(drives, inverse, HIGH)
        current = traces_now
        for p in range(NG):
            fresh = jnp.maximum(current + (drives - dot(current - traces_now, weights, HIGH)), 0.0)
            current = jnp.where(group32 == order[p], fresh, current)
        traces_now = current
        low = traces_now.astype(BF16)

        stage_traces(r + 1, low)
        to_neighbours(3 + r, tl_out.at[r + 1], tl_out.at[r + 1], lambda s: tl_in.at[r + 1, s])
        corr = lax.dot_general(
            traces_now, traces_now, (((0,), (0,)), ((), ())), precision=HIGH, preferred_element_type=F32
        )
        sq = [jnp.sum(bts[c] * bts[c], axis=0, keepdims=True) for c in range(2)]
        corr_out[r, 0:G, :] = fold_diagonal(corr)
        corr_out[r, G : G + 4, :] = jnp.broadcast_to(sq[0], (4, NC))
        corr_out[r, G + 4 : G + 8, :] = jnp.broadcast_to(sq[1], (4, NC))
        for d in range(1, NT):
            to = lax.rem(me + d, NT)
            send(corr_out.at[r], corr_in.at[r, me], tm_s.at[0, r, to], tm_r.at[0, r, me], (sp, to))

        lane = lanes(FR)
        spread = jnp.zeros((FR, NC), F32)
        for c in range(2):
            for s, part in enumerate(split3(bts[c])):
                spread = jnp.where(lane // 8 == s * 2 + c, part, spread)
        stacked = jnp.concatenate(
            [jnp.where(lane % 8 == b, spread, 0.0).astype(BF16) for b in range(8)], axis=0
        )
        eye = (
            lax.broadcasted_iota(jnp.int32, (48, NC), 0) == lax.broadcasted_iota(jnp.int32, (48, NC), 1)
        ).astype(F32).astype(BF16)
        btm[...] = dot_nt(eye, stacked).astype(BF16)
        vacc[...] = jnp.zeros_like(vacc)

        from_neighbours(3 + r, lambda s: tl_in.at[r + 1, s])
        residual(2 * r + 1, source, space, low, r + 1, r, True)

        row = lax.broadcasted_iota(jnp.int32, (FR, 48), 0)
        col = lax.broadcasted_iota(jnp.int32, (FR, 48), 1)
        summed = jnp.zeros((FR, 48), F32)
        for b in range(8):
            summed = summed + jnp.where(col % 8 == b, vacc[b * FR : (b + 1) * FR, :], 0.0)
        packed = jnp.zeros((FR, NC), F32)
        for c in range(2):
            total = jnp.sum(jnp.where((col // 8) % 2 == c, summed, 0.0), axis=1, keepdims=True)
            packed = jnp.where(lane == c, total, packed)
            field = space[c]
            squares = jnp.sum(jnp.sum(field * field, axis=0, keepdims=True), axis=1, keepdims=True)
            packed = jnp.where(lane == 2 + c, squares, packed)

        def level_send(i, value):
            q, rows = peers[i]
            vox[r, i, q] = value
            for other, oq in rows:
                send(vox.at[r, i, q], vox.at[r, i, q], vx_s.at[r, i, oq], vx_r.at[r, i, q], (other, me))

        def level_sum(i):
            q, rows = peers[i]
            for other, oq in rows:
                arrived(vox.at[r, i, oq], vx_s.at[r, i, oq], vx_r.at[r, i, oq], (other, me))
            total = vox[r, i, 0]
            for s in range(1, levels[i][1]):
                total = total + vox[r, i, s]
            return total

        level_send(0, packed)

        for d in range(1, NT):
            other = lax.rem(me + d, NT)
            arrived(corr_in.at[r, other], tm_s.at[0, r, other], tm_r.at[0, r, other], (sp, other))
        corr_in[r, me] = corr_out[r]
        total = corr_in[r, 0]
        for s in range(1, NT):
            total = total + corr_in[r, s]
        inverse_a = inverse_blocks(total[0:G], RIDGE_FOOT)
        square_time = [total[G : G + 1], total[G + 4 : G + 5]]
        masked = jnp.concatenate(
            [jnp.where(group32 == g, low.astype(F32), 0.0) for g in range(NG)], axis=0
        )
        z = dot_nt(inverse_a, masked, HIGH)
        z_high = z.astype(BF16)
        zs[0] = z_high
        zs[1] = (z - z_high.astype(F32)).astype(BF16)

        gather(2 * r + 1)

        def update_slice(s):
            k = s // 2
            rows = pl.ds(pl.multiple_of(lax.rem(s, 2) * 64, 64), 64)
            block = pieces[k]
            return dot(zs[0, rows, :], block) + dot(zs[1, rows, :], block)

        for d in range(1, NT):
            to = lax.rem(me + d, NT)
            sb[r, to, 0:64, :] = update_slice(to).astype(BF16)
            send(sb.at[r, to], rb.at[r, me], tm_s.at[1, r, to], tm_r.at[1, r, me], (sp, to))
        level_send(1, level_sum(0))
        total = update_slice(me)
        frame = sb[r, me, 64:80, :].astype(F32)
        for d in range(1, NT):
            other = lax.rem(me + d, NT)
            arrived(rb.at[r, other], tm_s.at[1, r, other], tm_r.at[1, r, other], (sp, other))
            total = total + rb[r, other, 0:64, :].astype(F32)
            frame = frame + rb[r, other, 64:80, :].astype(F32)
        my_k = me // 2
        my_rows = pl.ds(pl.multiple_of(lax.rem(me, 2) * 64, 64), 64)
        renewed = jnp.maximum(source[my_k, my_rows, :].astype(F32) + total, 0.0).astype(BF16)
        foot[r, my_k, my_rows, :] = renewed
        my_blocks = pl.ds(pl.multiple_of(me * 8, 8), 8)
        for c in range(2):
            scale = jnp.concatenate([square_time[c]] * (BV // NC), axis=1)
            bgs[r, c, my_blocks, :] = jnp.maximum(
                space[c, my_blocks, :] + frame[c * 8 : (c + 1) * 8] / (2.0 * scale), 0.0
            )
        for d in range(1, NT):
            to = lax.rem(me + d, NT)
            send(foot.at[r, my_k, my_rows], foot.at[r, my_k, my_rows], tm_s.at[2, r, to], tm_r.at[2, r, me], (sp, to))
            send(bgs.at[r, :, my_blocks], bgs.at[r, :, my_blocks], tm_s.at[3, r, to], tm_r.at[3, r, me], (sp, to))
        level_send(2, level_sum(1))
        for d in range(1, NT):
            other = lax.rem(me + d, NT)
            k = other // 2
            rows = pl.ds(pl.multiple_of(lax.rem(other, 2) * 64, 64), 64)
            blocks = pl.ds(pl.multiple_of(other * 8, 8), 8)
            arrived(foot.at[r, k, rows], tm_s.at[2, r, other], tm_r.at[2, r, other], (sp, other))
            arrived(bgs.at[r, :, blocks], tm_s.at[3, r, other], tm_r.at[3, r, other], (sp, other))
        if r + 1 < ROUNDS:
            stage_halo(r + 1, foot.at[r])
            to_neighbours(r + 1, halo_out.at[r + 1], halo_out.at[r + 1], lambda s: halo_f.at[r + 1, s])
        packed = level_sum(2)
        for c in range(2):
            change = packed[:, c : c + 1] / (2.0 * packed[:, 2 + c : 3 + c])
            bts[c] = jnp.maximum(bts[c] + jnp.broadcast_to(change, (FR, NC)), 0.0)

    out_tr[...] = traces_now
    out_f[...] = foot[ROUNDS - 1]
    out_bg[...] = bgs[ROUNDS - 1]
    out_bt[...] = bts[...]
    for copy in sends:
        copy.wait_send()


def solution(mesh):
    nsp = mesh.shape["space"]
    sizes = [2, min(4, nsp // 2), nsp // 2 // min(4, nsp // 2)]
    levels = ((1, sizes[0]), (2, sizes[1]), (2 * sizes[1], sizes[2]))
    vmem = pl.BlockSpec(memory_space=pltpu.VMEM)
    smem = pl.BlockSpec(memory_space=pltpu.SMEM)

    def body(activity, footprints, traces, bg_space, bg_time, block_lists, group_order):
        f0 = footprints[0].reshape(NC, BPG, BV).transpose(1, 0, 2)
        tr0 = traces[0].reshape(NC, FR).T
        bt0 = jnp.broadcast_to(bg_time[:, :, None], (2, FR, NC))
        out_tr, out_f, out_bg, out_bt = pl.pallas_call(
            functools.partial(kernel, nsp, levels),
            out_shape=(
                jax.ShapeDtypeStruct((FR, NC), F32),
                jax.ShapeDtypeStruct((BPG, NC, BV), BF16),
                jax.ShapeDtypeStruct((2, VB, BV), F32),
                jax.ShapeDtypeStruct((2, FR, NC), F32),
            ),
            in_specs=[vmem] * 5 + [smem] * 2,
            out_specs=(vmem,) * 4,
            scratch_shapes=[
                pltpu.VMEM((FR, BPG * NC), jnp.int32),
                pltpu.VMEM((2 * ROUNDS, EXT, FR, BV), BF16),
                pltpu.VMEM((BPG, NG * FR, BV), BF16),
                pltpu.VMEM((ROUNDS, BPG, NC, BV), BF16),
                pltpu.VMEM((ROUNDS, 2, VB, BV), F32),
                pltpu.VMEM((2, FR, NC), F32),
                pltpu.VMEM((ROUNDS, 2, NC, BV), BF16),
                pltpu.VMEM((ROUNDS, NC, BV), BF16),
                pltpu.VMEM((ROUNDS + 1, 2, FR + G, NC), BF16),
                pltpu.VMEM((ROUNDS + 1, FR + G, NC), BF16),
                pltpu.VMEM((ROUNDS, G + 8, NC), F32),
                pltpu.VMEM((ROUNDS, NT, G + 8, NC), F32),
                pltpu.VMEM((ROUNDS, NT, 80, BV), BF16),
                pltpu.VMEM((ROUNDS, NT, 80, BV), BF16),
                pltpu.VMEM((8 * FR, 48), F32),
                pltpu.VMEM((ROUNDS, 3, 4, FR, NC), F32),
                pltpu.VMEM((8, NC), F32),
                pltpu.VMEM((2, NC, NG * FR), BF16),
                pltpu.VMEM((48, 8 * FR), BF16),
                pltpu.SemaphoreType.DMA((9, 2)),
                pltpu.SemaphoreType.DMA((9, 2)),
                pltpu.SemaphoreType.DMA((4, ROUNDS, NT)),
                pltpu.SemaphoreType.DMA((4, ROUNDS, NT)),
                pltpu.SemaphoreType.DMA((ROUNDS, 3, 4)),
                pltpu.SemaphoreType.DMA((ROUNDS, 3, 4)),
            ],
            compiler_params=pltpu.CompilerParams(
                collective_id=0, has_side_effects=True, vmem_limit_bytes=48 * 1024 * 1024
            ),
        )(activity, f0, tr0, bg_space, bt0, block_lists[0], group_order[0])
        return (
            out_tr.T.reshape(1, NG, G, FR),
            out_f.transpose(1, 0, 2).reshape(1, NG, G, BPG, BV),
            out_bg,
            out_bt[:, :, 0],
        )

    return jax.shard_map(
        body,
        mesh=mesh,
        in_specs=(
            P("space", "tm", None),
            P("space", None, None, None, None),
            P("space", None, None, "tm"),
            P(None, "space", None),
            P(None, "tm"),
            P("space", None, None),
            P("space", None),
        ),
        out_specs=(
            P("space", None, None, "tm"),
            P("space", None, None, None, None),
            P(None, "space", None),
            P(None, "tm"),
        ),
        check_vma=False,
    )
```

```python
import functools

import jax
import jax.numpy as jnp
from jax import lax
from jax.experimental import pallas as pl
from jax.experimental.pallas import tpu as pltpu
from jax.sharding import PartitionSpec as P

MESH = pl.DeviceIdType.MESH
HIGH = lax.Precision.HIGHEST
F32 = jnp.float32
BF16 = jnp.bfloat16

G = 16
NG = 8
NC = NG * G
BPG = 4
BV = 512
VB = 64
EXT = 72
FR = 32
NT = 8
ROUNDS = 2
RIDGE_TRACE = 0.01 * BPG * BV
RIDGE_FOOT = 0.1 * FR * NT


def dot(a, b, precision=None):
    return lax.dot_general(a, b, (((1,), (0,)), ((), ())), precision=precision, preferred_element_type=F32)


def dot_nt(a, b, precision=None):
    return lax.dot_general(a, b, (((1,), (1,)), ((), ())), precision=precision, preferred_element_type=F32)


def split3(x):
    hi = x.astype(BF16).astype(F32)
    rest = x - hi
    mid = rest.astype(BF16).astype(F32)
    return hi, mid, rest - mid


def halves(x):
    high = x.astype(BF16)
    return high, (x - high.astype(F32)).astype(BF16)


def lanes(rows):
    return lax.broadcasted_iota(jnp.int32, (rows, NC), 1)


def fold_diagonal(square):
    group = lanes(G) // G
    out = jnp.zeros((G, NC), F32)
    for h in range(NG):
        out = out + jnp.where(group == h, square[h * G : (h + 1) * G], 0.0)
    return out


def spread_diagonal(folded):
    group = lanes(G) // G
    return jnp.concatenate([jnp.where(group == h, folded, 0.0) for h in range(NG)], axis=0)


def inverse_blocks(folded, ridge):
    first = lanes(G) % G
    sub = lax.broadcasted_iota(jnp.int32, (G, NC), 0)
    folded = folded + jnp.where(sub == first, ridge, 0.0)
    rows = []
    for n in range(G):
        moved = folded if n == 0 else pltpu.roll(folded, NC - n, 1)
        rows.append(jnp.where(first == 0, moved, jnp.where(sub == n, 1.0, 0.0)))
    for p in range(G):
        pivot = 1.0 / rows[p][p : p + 1]
        at = sub == p
        scaled = jnp.where(at, jnp.broadcast_to(pivot, (G, NC)), rows[p] * pivot)
        for n in range(G):
            if n != p:
                rows[n] = jnp.where(at, 0.0, rows[n]) - rows[n][p : p + 1] * scaled
        rows[p] = scaled
    out = jnp.zeros((G, NC), F32)
    for n in range(G):
        moved = rows[n] if n == 0 else pltpu.roll(rows[n], n, 1)
        out = jnp.where(first == n, moved, out)
    return spread_diagonal(out)


def kernel(
    nsp, levels,
    act_hbm, f0, tr_hbm, bg_hbm, bt_hbm, bl, order,
    out_tr, out_f, out_bg, out_bt,
    act, bg0, tr0, bt0, blrow, res, pieces, foot, bgs, bts, halo_f, halo_out, halo_row, tl_in, tl_out, dr_out, dr_in, corr_out, corr_in,
    part_out, part_in, edge_in, edge_pieces, edge_out, edge_sum, frame_out, frame_in, vacc, vox, zs, btm,
    in_sem, nb_s, nb_r, tm_s, tm_r, vx_s, vx_r,
):
    loads = [
        pltpu.make_async_copy(there, here, in_sem.at[i])
        for i, (there, here) in enumerate(
            ((tr_hbm, tr0), (bt_hbm, bt0), (bg_hbm, bg0), (act_hbm, act))
        )
    ]
    for load in loads:
        load.start()
    me = lax.axis_index("tm")
    sp = lax.axis_index("space")
    left = lax.rem(sp + nsp - 1, nsp)
    right = lax.rem(sp + 1, nsp)
    peers = []
    for stride, size in levels:
        q = lax.rem(sp // stride, size)
        row = []
        for d in range(1, size):
            other = lax.rem(q + d, size)
            row.append((sp + (other - q) * stride, other))
        peers.append((q, row))

    barrier = pltpu.get_barrier_semaphore()
    count = 0
    for d in range(1, NT):
        pl.semaphore_signal(barrier, inc=1, device_id=(sp, lax.rem(me + d, NT)), device_id_type=MESH)
        count += 1
    for other in (left, right):
        pl.semaphore_signal(barrier, inc=1, device_id=(other, me), device_id_type=MESH)
        count += 1
    for _, row in peers:
        for other, _ in row:
            pl.semaphore_signal(barrier, inc=1, device_id=(other, me), device_id_type=MESH)
            count += 1

    sends = []

    def send(src, dst, ssem, rsem, device):
        copy = pltpu.make_async_remote_copy(
            src_ref=src, dst_ref=dst, send_sem=ssem, recv_sem=rsem, device_id=device, device_id_type=MESH
        )
        copy.start()
        sends.append(copy)

    def arrived(ref, ssem, rsem, device):
        pltpu.make_async_remote_copy(
            src_ref=ref, dst_ref=ref, send_sem=ssem, recv_sem=rsem, device_id=device, device_id_type=MESH
        ).wait_recv()

    def to_neighbours(cat, src_left, src_right, dst):
        send(src_right, dst(0), nb_s.at[cat, 0], nb_r.at[cat, 0], (right, me))
        send(src_left, dst(1), nb_s.at[cat, 1], nb_r.at[cat, 1], (left, me))

    def from_neighbours(cat, dst):
        arrived(dst(0), nb_s.at[cat, 0], nb_r.at[cat, 0], (left, me))
        arrived(dst(1), nb_s.at[cat, 1], nb_r.at[cat, 1], (right, me))

    def to_frames(kind, r, src, dst):
        for d in range(1, NT):
            to = lax.rem(me + d, NT)
            send(src(to), dst(me), tm_s.at[kind, r, to], tm_r.at[kind, r, me], (sp, to))

    def from_frames(kind, r, dst):
        for d in range(1, NT):
            other = lax.rem(me + d, NT)
            arrived(dst(other), tm_s.at[kind, r, other], tm_r.at[kind, r, other], (sp, other))

    def group_rows(i):
        return pl.ds(pl.multiple_of(i * G, G), G)

    entry = [[bl[k, g] for k in range(BPG)] for g in range(NG)]
    group32 = lanes(FR) // G

    for k in range(BPG):
        row = jnp.zeros((FR, NC), jnp.int32)
        for g in range(NG):
            row = jnp.where(group32 == g, entry[g][k], row)
        blrow[:, k * NC : (k + 1) * NC] = row
    halo_id = jnp.full((G, NC), -1, jnp.int32)
    halo_k, halo_any, halo_at = [], [], []
    group16 = lanes(G) // G
    for g in range(NG):
        hid = jnp.int32(-1)
        hk = jnp.int32(0)
        for k in range(BPG):
            out = jnp.logical_or(entry[g][k] < 4, entry[g][k] >= 68)
            hid = jnp.where(out, entry[g][k], hid)
            hk = jnp.where(out, k, hk)
        halo_id = jnp.where(group16 == g, hid, halo_id)
        halo_k.append(hk)
        halo_any.append(hid >= 0)
        halo_at.append(jnp.where(hid >= 68, hid - 64, jnp.maximum(hid, 0)))
    halo_bf = halo_id.astype(F32).astype(BF16)

    def stage_traces(i, low):
        tl_out[i, 0:FR, :] = low
        tl_out[i, FR : FR + G, :] = halo_bf

    def gram_of(source):
        everything = source[...].reshape(BPG * NC, BV)
        total = jnp.zeros((NC, NC), F32)
        for k in range(BPG):
            product = dot_nt(source[k], everything)
            column = jnp.concatenate([jnp.full((G, NC), entry[g][k], jnp.int32) for g in range(NG)], axis=0)
            for j in range(BPG):
                row = blrow[:, j * NC : (j + 1) * NC]
                row = jnp.concatenate([row] * (NC // FR), axis=0)
                total = total + jnp.where(column == row, product[:, j * NC : (j + 1) * NC], 0.0)
        return total

    def field(r, j):
        if r == 0:
            rows = pl.ds(pl.multiple_of(8 * j, 8), 8)
            return jnp.concatenate([bg0[0, rows, :], bg0[1, rows, :]], axis=0)
        return bgs[r - 1, j].astype(F32)

    def chunk(inst, j, source, low4, traces_i, r, side, drive):
        parts = []
        for i in range(8):
            parts.append(jnp.where(blrow[...] == 8 * j + 4 + i, low4, 0.0).astype(BF16))
        lhs = jnp.concatenate(parts, axis=0)
        rebuilt = dot(lhs, source[...].reshape(BPG * NC, BV))
        if side is not None:
            low = tl_in[traces_i, side, 0:FR, :].astype(F32)
            hid = tl_in[traces_i, side, FR : FR + G, :].astype(F32)
            hid = jnp.concatenate([hid, hid], axis=0)
            base = 68.0 if side == 0 else 0.0
            near = jnp.concatenate(
                [jnp.where(hid == base + i, low, 0.0).astype(BF16) for i in range(4)], axis=0
            )
            near = dot(near, halo_f[r, side])
            edge = slice(0, 4) if side == 0 else slice(4, 8)
            if side == 0:
                rebuilt = jnp.concatenate([rebuilt[: 4 * FR] + near, rebuilt[4 * FR :]], axis=0)
            else:
                rebuilt = jnp.concatenate([rebuilt[: 4 * FR], rebuilt[4 * FR :] + near], axis=0)
        t0 = jnp.concatenate([bts[0]] * (BV // NC), axis=1)
        t1 = jnp.concatenate([bts[1]] * (BV // NC), axis=1)
        s = field(r, j)
        s0, s1 = s[0:8], s[8:16]
        out = []
        for i in range(8):
            backdrop = s0[i : i + 1] * t0 + s1[i : i + 1] * t1
            seen = act[8 * j + i].astype(F32)
            value = ((seen - rebuilt[i * FR : (i + 1) * FR]) - backdrop).astype(BF16)
            res[inst, 8 * j + 4 + i] = value
            out.append(value)
        if side is not None and drive:
            flat = jnp.concatenate(out[edge], axis=0)
            back = dot_nt(flat, halo_f[r, side])
            total = jnp.zeros((FR, NC), F32)
            for i in range(4):
                total = total + jnp.where(hid == base + i, back[i * FR : (i + 1) * FR], 0.0)
            dr_out[r, side] = total

    def background(inst, r):
        def body(j, carry):
            flat = res[inst, pl.ds(8 * j + 4, 8)].reshape(8 * FR, BV)
            frame = dot(btm[...], flat)
            frame_out[r, j] = (frame[0:16] + frame[16:32] + frame[32:48]).astype(BF16)
            s = jnp.concatenate([x.astype(BF16) for x in split3(field(r, j))], axis=0)
            vacc[...] += dot_nt(flat, s)
            return carry

        lax.fori_loop(0, 8, body, 0)

    def middle(inst, source, low4, r, start, stop):
        def body(j, carry):
            chunk(inst, j, source, low4, None, r, None, False)
            return carry

        lax.fori_loop(start, stop, body, 0)

    def edges(inst, source, low4, traces_i, r, drive):
        chunk(inst, 0, source, low4, traces_i, r, 0, drive)
        chunk(inst, 7, source, low4, traces_i, r, 1, drive)

    def four(low):
        return jnp.concatenate([low.astype(F32)] * BPG, axis=1)

    def gather(inst):
        for g in range(NG):
            for k in range(BPG):
                pieces[k, g * FR : (g + 1) * FR, :] = res[inst, entry[g][k]]

    loads[0].wait()
    loads[1].wait()
    eye32 = jnp.where(
        lax.broadcasted_iota(jnp.int32, (FR, FR), 0) == lax.broadcasted_iota(jnp.int32, (FR, FR), 1), 1.0, 0.0
    )
    eye = jnp.where(lax.broadcasted_iota(jnp.int32, (NC, NC), 0) == lanes(NC), 1.0, 0.0)
    traces_now = dot_nt(eye32, tr0[...], HIGH)
    for c in range(2):
        bts[c] = dot_nt(eye32, jnp.broadcast_to(bt0[c : c + 1, :], (NC, FR)), HIGH)
    low = traces_now.astype(BF16)
    for g in range(NG):
        halo_out[g * G : (g + 1) * G, :] = f0[halo_k[g], g * G : (g + 1) * G, :]
    stage_traces(0, low)
    for i in range(2 * ROUNDS):
        res[i, 0:4] = jnp.zeros((4, FR, BV), BF16)
        res[i, 68:72] = jnp.zeros((4, FR, BV), BF16)

    pl.semaphore_wait(barrier, count)
    to_neighbours(0, halo_out, halo_out, lambda s: halo_f.at[0, s])
    to_neighbours(2, tl_out.at[0], tl_out.at[0], lambda s: tl_in.at[0, s])

    for r in range(ROUNDS):
        source = f0 if r == 0 else foot.at[0]
        gram = gram_of(source)
        inverse = inverse_blocks(fold_diagonal(gram), RIDGE_TRACE)
        weights = dot(gram, inverse, HIGH)

        if r == 0:
            loads[2].wait()
            loads[3].wait()
        middle(2 * r, source, four(low), r, 1, 7)
        if r == 0:
            from_neighbours(0, lambda s: halo_f.at[0, s])
            from_neighbours(2, lambda s: tl_in.at[0, s])
        else:
            for side in range(2):
                from_frames(6 + side, r - 1, lambda at, side=side: halo_f.at[r, side, group_rows(at)])
        edges(2 * r, source, four(low), r, r, True)
        to_neighbours(5 + 2 * r, dr_out.at[r, 0], dr_out.at[r, 1], lambda s: dr_in.at[r, s])
        gather(2 * r)
        cross = jnp.zeros((NG * FR, NC), F32)
        for k in range(BPG):
            cross = cross + dot_nt(pieces[k], source[k])
        drives = jnp.zeros((FR, NC), F32)
        for g in range(NG):
            drives = drives + jnp.where(group32 == g, cross[g * FR : (g + 1) * FR], 0.0)
        from_neighbours(5 + 2 * r, lambda s: dr_in.at[r, s])
        drives = drives + (dr_in[r, 0] + dr_in[r, 1])
        drives = dot(drives, inverse, HIGH)
        high, rest = halves(weights)
        weights = jnp.concatenate([high, high, rest], axis=0)
        current = traces_now
        for p in range(NG):
            high, rest = halves(current - traces_now)
            coupled = dot(jnp.concatenate([high, rest, high], axis=1), weights)
            fresh = jnp.maximum(current + (drives - coupled), 0.0)
            current = jnp.where(group32 == order[p], fresh, current)
        traces_now = current
        low = traces_now.astype(BF16)

        stage_traces(r + 1, low)
        to_neighbours(3 + r, tl_out.at[r + 1], tl_out.at[r + 1], lambda s: tl_in.at[r + 1, s])
        corr = lax.dot_general(
            traces_now, traces_now, (((0,), (0,)), ((), ())), precision=HIGH, preferred_element_type=F32
        )
        sq = [jnp.sum(bts[c] * bts[c], axis=0, keepdims=True) for c in range(2)]
        corr_out[r, 0:G, :] = fold_diagonal(corr)
        corr_out[r, G : G + 4, :] = jnp.broadcast_to(sq[0], (4, NC))
        corr_out[r, G + 4 : G + 8, :] = jnp.broadcast_to(sq[1], (4, NC))
        to_frames(0, r, lambda to: corr_out.at[r], lambda at: corr_in.at[r, at])

        inst = 2 * r + 1
        middle(inst, source, four(low), r, 1, 7)
        from_neighbours(3 + r, lambda s: tl_in.at[r + 1, s])
        edges(inst, source, four(low), r + 1, r, False)
        cat = 5 + inst
        to_neighbours(
            cat, res.at[inst, pl.ds(4, 4)], res.at[inst, pl.ds(64, 4)], lambda s: edge_in.at[r, pl.ds(4 * s, 4)]
        )

        from_frames(0, r, lambda at: corr_in.at[r, at])
        corr_in[r, me] = corr_out[r]
        total = corr_in[r, 0]
        for s in range(1, NT):
            total = total + corr_in[r, s]
        inverse_a = inverse_blocks(total[0:G], RIDGE_FOOT)
        square_time = [total[G : G + 1], total[G + 4 : G + 5]]
        masked = jnp.concatenate(
            [jnp.where(group32 == g, low.astype(F32), 0.0) for g in range(NG)], axis=0
        )
        z = dot_nt(inverse_a, masked, HIGH)
        z_high = z.astype(BF16)
        zs[0] = z_high
        zs[1] = (z - z_high.astype(F32)).astype(BF16)

        gather(inst)
        for k in range(BPG):
            part_out[r, k] = (dot(zs[0], pieces[k]) + dot(zs[1], pieces[k])).astype(BF16)
        to_frames(1, r, lambda to: part_out.at[r, :, group_rows(to)], lambda at: part_in.at[r, at])

        lane = lanes(FR)
        spread = jnp.zeros((FR, NC), F32)
        for c in range(2):
            for s, part in enumerate(split3(bts[c])):
                spread = jnp.where(lane // 8 == s * 2 + c, part, spread)
        stacked = jnp.concatenate(
            [jnp.where(lane % 8 == b, spread, 0.0).astype(BF16) for b in range(8)], axis=0
        )
        btm[...] = dot_nt(eye[0:48].astype(BF16), stacked).astype(BF16)
        vacc[...] = jnp.zeros_like(vacc)

        background(inst, r)
        to_frames(3, r, lambda to: frame_out.at[r, to], lambda at: frame_in.at[r, at])

        row = lax.broadcasted_iota(jnp.int32, (FR, 48), 0)
        col = lax.broadcasted_iota(jnp.int32, (FR, 48), 1)
        summed = jnp.zeros((FR, 48), F32)
        for b in range(8):
            summed = summed + jnp.where(col % 8 == b, vacc[b * FR : (b + 1) * FR, :], 0.0)
        packed = jnp.zeros((FR, NC), F32)
        for c in range(2):
            total = jnp.sum(jnp.where((col // 8) % 2 == c, summed, 0.0), axis=1, keepdims=True)
            packed = jnp.where(lane == c, total, packed)
            squares = jnp.zeros((8, BV), F32)
            for j in range(8):
                part = field(r, j)[c * 8 : (c + 1) * 8]
                squares = squares + part * part
            squares = jnp.sum(jnp.sum(squares, axis=0, keepdims=True), axis=1, keepdims=True)
            packed = jnp.where(lane == 2 + c, squares, packed)

        def level_send(i, value):
            q, rows = peers[i]
            vox[r, i, q] = value
            for other, oq in rows:
                send(vox.at[r, i, q], vox.at[r, i, q], vx_s.at[r, i, oq], vx_r.at[r, i, q], (other, me))

        def level_sum(i):
            q, rows = peers[i]
            for other, oq in rows:
                arrived(vox.at[r, i, oq], vx_s.at[r, i, oq], vx_r.at[r, i, oq], (other, me))
            total = vox[r, i, 0]
            for s in range(1, levels[i][1]):
                total = total + vox[r, i, s]
            return total

        level_send(0, dot_nt(eye[0:8], packed, HIGH))

        from_neighbours(cat, lambda s: edge_in.at[r, pl.ds(4 * s, 4)])
        for g in range(NG):
            block = edge_in[r, halo_at[g]]
            edge_pieces[g * FR : (g + 1) * FR, :] = jnp.where(halo_any[g], block.astype(F32), 0.0).astype(BF16)
        edge_out[r] = (dot(zs[0], edge_pieces[...]) + dot(zs[1], edge_pieces[...])).astype(BF16)
        to_frames(2, r, lambda to: edge_out.at[r, group_rows(to)], lambda at: edge_sum.at[r, at])

        level_send(1, level_sum(0))

        frame = frame_out[r, me].astype(F32)
        from_frames(3, r, lambda at: frame_in.at[r, at])
        for d in range(1, NT):
            frame = frame + frame_in[r, lax.rem(me + d, NT)].astype(F32)
        scale = jnp.concatenate([jnp.broadcast_to(square_time[c], (8, NC)) for c in range(2)], axis=0)
        scale = jnp.concatenate([scale] * (BV // NC), axis=1)
        bgs[r, me] = jnp.maximum(field(r, me) + frame / (2.0 * scale), 0.0).astype(BF16)
        to_frames(5, r, lambda to: bgs.at[r, me], lambda at: bgs.at[r, at])
        my_rows = group_rows(me)
        total = part_out[r, :, my_rows].astype(F32)
        from_frames(1, r, lambda at: part_in.at[r, at])
        for d in range(1, NT):
            total = total + part_in[r, lax.rem(me + d, NT)].astype(F32)
        from_frames(2, r, lambda at: edge_sum.at[r, at])
        extra = edge_out[r, my_rows].astype(F32)
        for d in range(1, NT):
            extra = extra + edge_sum[r, lax.rem(me + d, NT)].astype(F32)
        for k in range(BPG):
            mine = bl[k, me]
            outside = jnp.logical_or(mine < 4, mine >= 68)
            moved = total[k] + jnp.where(outside, extra, 0.0)
            fresh = jnp.maximum(source[k, my_rows, :].astype(F32) + moved, 0.0)
            foot[r, k, my_rows, :] = fresh.astype(BF16)
            spill = fresh if k == 0 else jnp.where(outside, fresh, spill)
        last = r + 1 == ROUNDS
        if not last:
            halo_row[...] = spill.astype(BF16)
            to_neighbours(1, halo_row, halo_row, lambda s: halo_f.at[r + 1, s, my_rows])
        to_frames(4, r, lambda to: foot.at[r, :, my_rows], lambda at: foot.at[r, :, group_rows(at)])
        if not last:
            from_neighbours(1, lambda s: halo_f.at[r + 1, s, my_rows])
            for side in range(2):
                to_frames(
                    6 + side,
                    r,
                    lambda to, side=side: halo_f.at[r + 1, side, my_rows],
                    lambda at, side=side: halo_f.at[r + 1, side, group_rows(at)],
                )
        from_frames(5, r, lambda at: bgs.at[r, at])
        from_frames(4, r, lambda at: foot.at[r, :, group_rows(at)])
        packed = level_sum(1)
        for c in range(2):
            change = packed[c : c + 1] / (2.0 * packed[2 + c : 3 + c])
            change = dot_nt(eye32, jnp.broadcast_to(change, (NC, FR)), HIGH)
            bts[c] = jnp.maximum(bts[c] + change, 0.0)

    out_tr[...] = dot_nt(eye, traces_now, HIGH)
    out_f[...] = foot[ROUNDS - 1]
    out_bg[...] = bgs[ROUNDS - 1]
    both = jnp.where(lanes(FR) == 0, bts[0], jnp.where(lanes(FR) == 1, bts[1], 0.0))
    out_bt[...] = dot_nt(eye[0:8], both, HIGH)[0:2]
    for copy in sends:
        copy.wait_send()


def solution(mesh):
    nsp = mesh.shape["space"]
    near = min(8, nsp)
    levels = ((1, near), (near, nsp // near))
    vmem = pl.BlockSpec(memory_space=pltpu.VMEM)
    far = pl.BlockSpec(memory_space=pltpu.HBM)
    smem = pl.BlockSpec(memory_space=pltpu.SMEM)

    def body(activity, footprints, traces, bg_space, bg_time, block_lists, group_order):
        f0 = footprints[0].reshape(NC, BPG, BV).transpose(1, 0, 2)
        tr0 = traces.reshape(NC, FR)
        out_tr, out_f, out_bg, out_bt = pl.pallas_call(
            functools.partial(kernel, nsp, levels),
            out_shape=(
                jax.ShapeDtypeStruct((NC, FR), F32),
                jax.ShapeDtypeStruct((BPG, NC, BV), BF16),
                jax.ShapeDtypeStruct((8, 16, BV), BF16),
                jax.ShapeDtypeStruct((2, FR), F32),
            ),
            in_specs=[far, vmem, far, far, far, smem, smem],
            out_specs=(vmem,) * 4,
            scratch_shapes=[
                pltpu.VMEM((VB, FR, BV), BF16),
                pltpu.VMEM((2, VB, BV), F32),
                pltpu.VMEM((NC, FR), F32),
                pltpu.VMEM((2, FR), F32),
                pltpu.VMEM((FR, BPG * NC), jnp.int32),
                pltpu.VMEM((2 * ROUNDS, EXT, FR, BV), BF16),
                pltpu.VMEM((BPG, NG * FR, BV), BF16),
                pltpu.VMEM((ROUNDS, BPG, NC, BV), BF16),
                pltpu.VMEM((ROUNDS, 8, 16, BV), BF16),
                pltpu.VMEM((2, FR, NC), F32),
                pltpu.VMEM((ROUNDS, 2, NC, BV), BF16),
                pltpu.VMEM((NC, BV), BF16),
                pltpu.VMEM((G, BV), BF16),
                pltpu.VMEM((ROUNDS + 1, 2, FR + G, NC), BF16),
                pltpu.VMEM((ROUNDS + 1, FR + G, NC), BF16),
                pltpu.VMEM((ROUNDS, 2, FR, NC), F32),
                pltpu.VMEM((ROUNDS, 2, FR, NC), F32),
                pltpu.VMEM((ROUNDS, G + 8, NC), F32),
                pltpu.VMEM((ROUNDS, NT, G + 8, NC), F32),
                pltpu.VMEM((ROUNDS, BPG, NC, BV), BF16),
                pltpu.VMEM((ROUNDS, NT, BPG, G, BV), BF16),
                pltpu.VMEM((ROUNDS, 8, FR, BV), BF16),
                pltpu.VMEM((NG * FR, BV), BF16),
                pltpu.VMEM((ROUNDS, NC, BV), BF16),
                pltpu.VMEM((ROUNDS, NT, G, BV), BF16),
                pltpu.VMEM((ROUNDS, NT, 16, BV), BF16),
                pltpu.VMEM((ROUNDS, NT, 16, BV), BF16),
                pltpu.VMEM((8 * FR, 48), F32),
                pltpu.VMEM((ROUNDS, 2, 8, 8, FR), F32),
                pltpu.VMEM((2, NC, NG * FR), BF16),
                pltpu.VMEM((48, 8 * FR), BF16),
                pltpu.SemaphoreType.DMA((4,)),
                pltpu.SemaphoreType.DMA((9, 2)),
                pltpu.SemaphoreType.DMA((9, 2)),
                pltpu.SemaphoreType.DMA((8, ROUNDS, NT)),
                pltpu.SemaphoreType.DMA((8, ROUNDS, NT)),
                pltpu.SemaphoreType.DMA((ROUNDS, 2, 8)),
                pltpu.SemaphoreType.DMA((ROUNDS, 2, 8)),
            ],
            compiler_params=pltpu.CompilerParams(
                collective_id=0, has_side_effects=True, vmem_limit_bytes=52 * 1024 * 1024
            ),
        )(activity, f0, tr0, bg_space, bg_time, block_lists[0].T, group_order[0])
        return (
            out_tr.reshape(1, NG, G, FR),
            out_f.transpose(1, 0, 2).reshape(1, NG, G, BPG, BV),
            out_bg.reshape(8, 2, 8, BV).transpose(1, 0, 2, 3).reshape(2, VB, BV).astype(F32),
            out_bt,
        )

    return jax.shard_map(
        body,
        mesh=mesh,
        in_specs=(
            P("space", "tm", None),
            P("space", None, None, None, None),
            P("space", None, None, "tm"),
            P(None, "space", None),
            P(None, "tm"),
            P("space", None, None),
            P("space", None),
        ),
        out_specs=(
            P("space", None, None, "tm"),
            P("space", None, None, None, None),
            P(None, "space", None),
            P(None, "tm"),
        ),
        check_vma=False,
    )
```

```python
import functools

import jax
import jax.numpy as jnp
from jax import lax
from jax.experimental import pallas as pl
from jax.experimental.pallas import tpu as pltpu
from jax.sharding import PartitionSpec as P

MESH = pl.DeviceIdType.MESH
HIGH = lax.Precision.HIGHEST
F32 = jnp.float32
BF16 = jnp.bfloat16

G = 16
NG = 8
NC = NG * G
BPG = 4
BV = 512
VB = 64
EXT = 72
FR = 32
NT = 8
ROUNDS = 2
RIDGE_TRACE = 0.01 * BPG * BV
RIDGE_FOOT = 0.1 * FR * NT


def dot(a, b, precision=None):
    return lax.dot_general(a, b, (((1,), (0,)), ((), ())), precision=precision, preferred_element_type=F32)


def dot_nt(a, b, precision=None):
    return lax.dot_general(a, b, (((1,), (1,)), ((), ())), precision=precision, preferred_element_type=F32)


def split3(x):
    hi = x.astype(BF16).astype(F32)
    rest = x - hi
    mid = rest.astype(BF16).astype(F32)
    return hi, mid, rest - mid


def halves(x):
    high = x.astype(BF16)
    return high, (x - high.astype(F32)).astype(BF16)


def lanes(rows):
    return lax.broadcasted_iota(jnp.int32, (rows, NC), 1)


def fold_diagonal(square):
    group = lanes(G) // G
    out = jnp.zeros((G, NC), F32)
    for h in range(NG):
        out = out + jnp.where(group == h, square[h * G : (h + 1) * G], 0.0)
    return out


def spread_diagonal(folded):
    group = lanes(G) // G
    return jnp.concatenate([jnp.where(group == h, folded, 0.0) for h in range(NG)], axis=0)


def inverse_blocks(folded, ridge):
    first = lanes(G) % G
    sub = lax.broadcasted_iota(jnp.int32, (G, NC), 0)
    folded = folded + jnp.where(sub == first, ridge, 0.0)
    rows = []
    for n in range(G):
        moved = folded if n == 0 else pltpu.roll(folded, NC - n, 1)
        rows.append(jnp.where(first == 0, moved, jnp.where(sub == n, 1.0, 0.0)))
    for p in range(G):
        pivot = 1.0 / rows[p][p : p + 1]
        at = sub == p
        scaled = jnp.where(at, jnp.broadcast_to(pivot, (G, NC)), rows[p] * pivot)
        for n in range(G):
            if n != p:
                rows[n] = jnp.where(at, 0.0, rows[n]) - rows[n][p : p + 1] * scaled
        rows[p] = scaled
    out = jnp.zeros((G, NC), F32)
    for n in range(G):
        moved = rows[n] if n == 0 else pltpu.roll(rows[n], n, 1)
        out = jnp.where(first == n, moved, out)
    return spread_diagonal(out)


def kernel(
    nsp, levels,
    act_hbm, f0, tr_hbm, bg_hbm, bt_hbm, bl, order,
    out_tr, out_f, out_bg, out_bt,
    act, bg0, tr0, bt0, blrow, res, pieces, foot, bgs, bts, halo_f, halo_out, halo_row, tl_in, tl_out, dr_out, dr_in, corr_out, corr_in,
    part_out, part_in, edge_in, edge_pieces, edge_out, edge_sum, frame_out, frame_in, vacc, vox, zs, btm,
    in_sem, nb_s, nb_r, tm_s, tm_r, vx_s, vx_r,
):
    loads = [
        pltpu.make_async_copy(there, here, in_sem.at[i])
        for i, (there, here) in enumerate(
            ((tr_hbm, tr0), (bt_hbm, bt0), (bg_hbm, bg0), (act_hbm, act))
        )
    ]
    for load in loads:
        load.start()
    me = lax.axis_index("tm")
    sp = lax.axis_index("space")
    left = lax.rem(sp + nsp - 1, nsp)
    right = lax.rem(sp + 1, nsp)
    peers = []
    for stride, size in levels:
        q = lax.rem(sp // stride, size)
        row = []
        for d in range(1, size):
            other = lax.rem(q + d, size)
            row.append((sp + (other - q) * stride, other))
        peers.append((q, row))

    barrier = pltpu.get_barrier_semaphore()
    count = 0
    for d in range(1, NT):
        pl.semaphore_signal(barrier, inc=1, device_id=(sp, lax.rem(me + d, NT)), device_id_type=MESH)
        count += 1
    for other in (left, right):
        pl.semaphore_signal(barrier, inc=1, device_id=(other, me), device_id_type=MESH)
        count += 1
    for _, row in peers:
        for other, _ in row:
            pl.semaphore_signal(barrier, inc=1, device_id=(other, me), device_id_type=MESH)
            count += 1

    sends = []

    def send(src, dst, ssem, rsem, device):
        copy = pltpu.make_async_remote_copy(
            src_ref=src, dst_ref=dst, send_sem=ssem, recv_sem=rsem, device_id=device, device_id_type=MESH
        )
        copy.start()
        sends.append(copy)

    def arrived(ref, ssem, rsem, device):
        pltpu.make_async_remote_copy(
            src_ref=ref, dst_ref=ref, send_sem=ssem, recv_sem=rsem, device_id=device, device_id_type=MESH
        ).wait_recv()

    def to_neighbours(cat, src_left, src_right, dst):
        send(src_right, dst(0), nb_s.at[cat, 0], nb_r.at[cat, 0], (right, me))
        send(src_left, dst(1), nb_s.at[cat, 1], nb_r.at[cat, 1], (left, me))

    def from_neighbours(cat, dst):
        arrived(dst(0), nb_s.at[cat, 0], nb_r.at[cat, 0], (left, me))
        arrived(dst(1), nb_s.at[cat, 1], nb_r.at[cat, 1], (right, me))

    def to_frames(kind, r, src, dst):
        for d in range(1, NT):
            to = lax.rem(me + d, NT)
            send(src(to), dst(me), tm_s.at[kind, r, to], tm_r.at[kind, r, me], (sp, to))

    def from_frames(kind, r, dst):
        for d in range(1, NT):
            other = lax.rem(me + d, NT)
            arrived(dst(other), tm_s.at[kind, r, other], tm_r.at[kind, r, other], (sp, other))

    def group_rows(i):
        return pl.ds(pl.multiple_of(i * G, G), G)

    entry = [[bl[k, g] for k in range(BPG)] for g in range(NG)]
    group32 = lanes(FR) // G

    for k in range(BPG):
        row = jnp.zeros((FR, NC), jnp.int32)
        for g in range(NG):
            row = jnp.where(group32 == g, entry[g][k], row)
        blrow[:, k * NC : (k + 1) * NC] = row
    halo_id = jnp.full((G, NC), -1, jnp.int32)
    halo_k, halo_any, halo_at = [], [], []
    group16 = lanes(G) // G
    for g in range(NG):
        hid = jnp.int32(-1)
        hk = jnp.int32(0)
        for k in range(BPG):
            out = jnp.logical_or(entry[g][k] < 4, entry[g][k] >= 68)
            hid = jnp.where(out, entry[g][k], hid)
            hk = jnp.where(out, k, hk)
        halo_id = jnp.where(group16 == g, hid, halo_id)
        halo_k.append(hk)
        halo_any.append(hid >= 0)
        halo_at.append(jnp.where(hid >= 68, hid - 64, jnp.maximum(hid, 0)))
    halo_bf = halo_id.astype(F32).astype(BF16)

    def stage_traces(i, low):
        tl_out[i, 0:FR, :] = low
        tl_out[i, FR : FR + G, :] = halo_bf

    def gram_of(source):
        everything = source[...].reshape(BPG * NC, BV)
        total = jnp.zeros((NC, NC), F32)
        for k in range(BPG):
            product = dot_nt(source[k], everything)
            column = jnp.concatenate([jnp.full((G, NC), entry[g][k], jnp.int32) for g in range(NG)], axis=0)
            for j in range(BPG):
                row = blrow[:, j * NC : (j + 1) * NC]
                row = jnp.concatenate([row] * (NC // FR), axis=0)
                total = total + jnp.where(column == row, product[:, j * NC : (j + 1) * NC], 0.0)
        return total

    def field(r, j):
        if r == 0:
            rows = pl.ds(pl.multiple_of(8 * j, 8), 8)
            return jnp.concatenate([bg0[0, rows, :], bg0[1, rows, :]], axis=0)
        return bgs[r - 1, j].astype(F32)

    def chunk(inst, j, source, low4, traces_i, r, side, drive):
        parts = []
        for i in range(8):
            parts.append(jnp.where(blrow[...] == 8 * j + 4 + i, low4, 0.0).astype(BF16))
        lhs = jnp.concatenate(parts, axis=0)
        rebuilt = dot(lhs, source[...].reshape(BPG * NC, BV))
        if side is not None:
            low = tl_in[traces_i, side, 0:FR, :].astype(F32)
            hid = tl_in[traces_i, side, FR : FR + G, :].astype(F32)
            hid = jnp.concatenate([hid, hid], axis=0)
            base = 68.0 if side == 0 else 0.0
            near = jnp.concatenate(
                [jnp.where(hid == base + i, low, 0.0).astype(BF16) for i in range(4)], axis=0
            )
            near = dot(near, halo_f[r, side])
            edge = slice(0, 4) if side == 0 else slice(4, 8)
            if side == 0:
                rebuilt = jnp.concatenate([rebuilt[: 4 * FR] + near, rebuilt[4 * FR :]], axis=0)
            else:
                rebuilt = jnp.concatenate([rebuilt[: 4 * FR], rebuilt[4 * FR :] + near], axis=0)
        t0 = jnp.concatenate([bts[0]] * (BV // NC), axis=1)
        t1 = jnp.concatenate([bts[1]] * (BV // NC), axis=1)
        s = field(r, j)
        s0, s1 = s[0:8], s[8:16]
        out = []
        for i in range(8):
            backdrop = s0[i : i + 1] * t0 + s1[i : i + 1] * t1
            seen = act[8 * j + i].astype(F32)
            value = ((seen - rebuilt[i * FR : (i + 1) * FR]) - backdrop).astype(BF16)
            res[inst, 8 * j + 4 + i] = value
            out.append(value)
        if side is not None and drive:
            flat = jnp.concatenate(out[edge], axis=0)
            back = dot_nt(flat, halo_f[r, side])
            total = jnp.zeros((FR, NC), F32)
            for i in range(4):
                total = total + jnp.where(hid == base + i, back[i * FR : (i + 1) * FR], 0.0)
            dr_out[r, side] = total

    def background(inst, r):
        def body(j, carry):
            flat = res[inst, pl.ds(8 * j + 4, 8)].reshape(8 * FR, BV)
            frame = dot(btm[...], flat)
            frame_out[r, j] = (frame[0:16] + frame[16:32] + frame[32:48]).astype(BF16)
            s = jnp.concatenate([x.astype(BF16) for x in split3(field(r, j))], axis=0)
            vacc[...] += dot_nt(flat, s)
            return carry

        lax.fori_loop(0, 8, body, 0)

    def middle(inst, source, low4, r, start, stop):
        def body(j, carry):
            chunk(inst, j, source, low4, None, r, None, False)
            return carry

        lax.fori_loop(start, stop, body, 0)

    def edges(inst, source, low4, traces_i, r, drive):
        chunk(inst, 0, source, low4, traces_i, r, 0, drive)
        chunk(inst, 7, source, low4, traces_i, r, 1, drive)

    def four(low):
        return jnp.concatenate([low.astype(F32)] * BPG, axis=1)

    def gather(inst):
        for g in range(NG):
            for k in range(BPG):
                pieces[k, g * FR : (g + 1) * FR, :] = res[inst, entry[g][k]]

    loads[0].wait()
    loads[1].wait()
    eye32 = jnp.where(
        lax.broadcasted_iota(jnp.int32, (FR, FR), 0) == lax.broadcasted_iota(jnp.int32, (FR, FR), 1), 1.0, 0.0
    )
    eye = jnp.where(lax.broadcasted_iota(jnp.int32, (NC, NC), 0) == lanes(NC), 1.0, 0.0)
    traces_now = dot_nt(eye32, tr0[...], HIGH)
    for c in range(2):
        bts[c] = dot_nt(eye32, jnp.broadcast_to(bt0[c : c + 1, :], (NC, FR)), HIGH)
    low = traces_now.astype(BF16)
    for g in range(NG):
        halo_out[g * G : (g + 1) * G, :] = f0[halo_k[g], g * G : (g + 1) * G, :]
    stage_traces(0, low)
    for i in range(2 * ROUNDS):
        res[i, 0:4] = jnp.zeros((4, FR, BV), BF16)
        res[i, 68:72] = jnp.zeros((4, FR, BV), BF16)

    pl.semaphore_wait(barrier, count)
    to_neighbours(0, halo_out, halo_out, lambda s: halo_f.at[0, s])
    to_neighbours(2, tl_out.at[0], tl_out.at[0], lambda s: tl_in.at[0, s])

    for r in range(ROUNDS):
        source = f0 if r == 0 else foot.at[0]
        gram = gram_of(source)
        inverse = inverse_blocks(fold_diagonal(gram), RIDGE_TRACE)
        weights = dot(gram, inverse, HIGH)

        if r == 0:
            loads[2].wait()
            loads[3].wait()
        middle(2 * r, source, four(low), r, 1, 7)
        if r == 0:
            from_neighbours(0, lambda s: halo_f.at[0, s])
            from_neighbours(2, lambda s: tl_in.at[0, s])
        else:
            for side in range(2):
                from_frames(6 + side, r - 1, lambda at, side=side: halo_f.at[r, side, group_rows(at)])
        edges(2 * r, source, four(low), r, r, True)
        to_neighbours(5 + 2 * r, dr_out.at[r, 0], dr_out.at[r, 1], lambda s: dr_in.at[r, s])
        gather(2 * r)
        cross = jnp.zeros((NG * FR, NC), F32)
        for k in range(BPG):
            cross = cross + dot_nt(pieces[k], source[k])
        drives = jnp.zeros((FR, NC), F32)
        for g in range(NG):
            drives = drives + jnp.where(group32 == g, cross[g * FR : (g + 1) * FR], 0.0)
        from_neighbours(5 + 2 * r, lambda s: dr_in.at[r, s])
        drives = drives + (dr_in[r, 0] + dr_in[r, 1])
        drives = dot(drives, inverse, HIGH)
        high, rest = halves(weights)
        weights = jnp.concatenate([high, high, rest], axis=0)
        current = traces_now
        for p in range(NG):
            high, rest = halves(current - traces_now)
            coupled = dot(jnp.concatenate([high, rest, high], axis=1), weights)
            fresh = jnp.maximum(current + (drives - coupled), 0.0)
            current = jnp.where(group32 == order[p], fresh, current)
        traces_now = current
        low = traces_now.astype(BF16)

        stage_traces(r + 1, low)
        to_neighbours(3 + r, tl_out.at[r + 1], tl_out.at[r + 1], lambda s: tl_in.at[r + 1, s])
        corr = lax.dot_general(
            traces_now, traces_now, (((0,), (0,)), ((), ())), precision=HIGH, preferred_element_type=F32
        )
        sq = [jnp.sum(bts[c] * bts[c], axis=0, keepdims=True) for c in range(2)]
        corr_out[r, 0:G, :] = fold_diagonal(corr)
        corr_out[r, G : G + 4, :] = jnp.broadcast_to(sq[0], (4, NC))
        corr_out[r, G + 4 : G + 8, :] = jnp.broadcast_to(sq[1], (4, NC))
        to_frames(0, r, lambda to: corr_out.at[r], lambda at: corr_in.at[r, at])

        inst = 2 * r + 1
        middle(inst, source, four(low), r, 1, 7)
        from_neighbours(3 + r, lambda s: tl_in.at[r + 1, s])
        edges(inst, source, four(low), r + 1, r, False)
        cat = 5 + inst
        to_neighbours(
            cat, res.at[inst, pl.ds(4, 4)], res.at[inst, pl.ds(64, 4)], lambda s: edge_in.at[r, pl.ds(4 * s, 4)]
        )

        from_frames(0, r, lambda at: corr_in.at[r, at])
        corr_in[r, me] = corr_out[r]
        total = corr_in[r, 0]
        for s in range(1, NT):
            total = total + corr_in[r, s]
        inverse_a = inverse_blocks(total[0:G], RIDGE_FOOT)
        square_time = [total[G : G + 1], total[G + 4 : G + 5]]
        masked = jnp.concatenate(
            [jnp.where(group32 == g, low.astype(F32), 0.0) for g in range(NG)], axis=0
        )
        z = dot_nt(inverse_a, masked, HIGH)
        z_high = z.astype(BF16)
        zs[0] = z_high
        zs[1] = (z - z_high.astype(F32)).astype(BF16)

        for g in range(NG):
            for k in range(BPG - 1):
                at = jnp.where(halo_k[g] <= k, entry[g][k + 1], entry[g][k])
                pieces[k, g * FR : (g + 1) * FR, :] = res[inst, at]
        for k in range(BPG - 1):
            part_out[r, k] = (dot(zs[0], pieces[k]) + dot(zs[1], pieces[k])).astype(BF16)
        to_frames(1, r, lambda to: part_out.at[r, :, group_rows(to)], lambda at: part_in.at[r, at])

        lane = lanes(FR)
        spread = jnp.zeros((FR, NC), F32)
        for c in range(2):
            for s, part in enumerate(split3(bts[c])):
                spread = jnp.where(lane // 8 == s * 2 + c, part, spread)
        stacked = jnp.concatenate(
            [jnp.where(lane % 8 == b, spread, 0.0).astype(BF16) for b in range(8)], axis=0
        )
        btm[...] = dot_nt(eye[0:48].astype(BF16), stacked).astype(BF16)
        vacc[...] = jnp.zeros_like(vacc)

        background(inst, r)
        to_frames(3, r, lambda to: frame_out.at[r, to], lambda at: frame_in.at[r, at])

        from_neighbours(cat, lambda s: edge_in.at[r, pl.ds(4 * s, 4)])
        for g in range(NG):
            block = edge_in[r, halo_at[g]]
            own = res[inst, jnp.where(halo_any[g], 4, entry[g][0])]
            edge_pieces[g * FR : (g + 1) * FR, :] = jnp.where(
                halo_any[g], block.astype(F32), own.astype(F32)
            ).astype(BF16)
        edge_out[r] = (dot(zs[0], edge_pieces[...]) + dot(zs[1], edge_pieces[...])).astype(BF16)
        to_frames(2, r, lambda to: edge_out.at[r, group_rows(to)], lambda at: edge_sum.at[r, at])

        row = lax.broadcasted_iota(jnp.int32, (FR, 48), 0)
        col = lax.broadcasted_iota(jnp.int32, (FR, 48), 1)
        summed = jnp.zeros((FR, 48), F32)
        for b in range(8):
            summed = summed + jnp.where(col % 8 == b, vacc[b * FR : (b + 1) * FR, :], 0.0)
        packed = jnp.zeros((FR, NC), F32)
        for c in range(2):
            total = jnp.sum(jnp.where((col // 8) % 2 == c, summed, 0.0), axis=1, keepdims=True)
            packed = jnp.where(lane == c, total, packed)
            squares = jnp.zeros((8, BV), F32)
            for j in range(8):
                part = field(r, j)[c * 8 : (c + 1) * 8]
                squares = squares + part * part
            squares = jnp.sum(jnp.sum(squares, axis=0, keepdims=True), axis=1, keepdims=True)
            packed = jnp.where(lane == 2 + c, squares, packed)

        def level_send(i, value):
            q, rows = peers[i]
            vox[r, i, q] = value
            for other, oq in rows:
                send(vox.at[r, i, q], vox.at[r, i, q], vx_s.at[r, i, oq], vx_r.at[r, i, q], (other, me))

        def level_sum(i):
            q, rows = peers[i]
            for other, oq in rows:
                arrived(vox.at[r, i, oq], vx_s.at[r, i, oq], vx_r.at[r, i, oq], (other, me))
            total = vox[r, i, 0]
            for s in range(1, levels[i][1]):
                total = total + vox[r, i, s]
            return total

        level_send(0, dot_nt(eye[0:8], packed, HIGH))

        frame = frame_out[r, me].astype(F32)
        from_frames(3, r, lambda at: frame_in.at[r, at])
        for d in range(1, NT):
            frame = frame + frame_in[r, lax.rem(me + d, NT)].astype(F32)
        scale = jnp.concatenate([jnp.broadcast_to(square_time[c], (8, NC)) for c in range(2)], axis=0)
        scale = jnp.concatenate([scale] * (BV // NC), axis=1)
        bgs[r, me] = jnp.maximum(field(r, me) + frame / (2.0 * scale), 0.0).astype(BF16)
        to_frames(5, r, lambda to: bgs.at[r, me], lambda at: bgs.at[r, at])
        my_rows = group_rows(me)
        total = part_out[r, :, my_rows].astype(F32)
        from_frames(1, r, lambda at: part_in.at[r, at])
        for d in range(1, NT):
            total = total + part_in[r, lax.rem(me + d, NT)].astype(F32)
        from_frames(2, r, lambda at: edge_sum.at[r, at])
        extra = edge_out[r, my_rows].astype(F32)
        for d in range(1, NT):
            extra = extra + edge_sum[r, lax.rem(me + d, NT)].astype(F32)
        which = jnp.int32(0)
        for k in range(BPG):
            mine = bl[k, me]
            which = jnp.where(jnp.logical_or(mine < 4, mine >= 68), k, which)
        for k in range(BPG):
            moved = jnp.where(which < k, total[max(k - 1, 0)], total[min(k, BPG - 2)])
            moved = jnp.where(which == k, extra, moved)
            fresh = jnp.maximum(source[k, my_rows, :].astype(F32) + moved, 0.0)
            foot[r, k, my_rows, :] = fresh.astype(BF16)
            spill = fresh if k == 0 else jnp.where(which == k, fresh, spill)
        last = r + 1 == ROUNDS
        if not last:
            halo_row[...] = spill.astype(BF16)
            to_neighbours(1, halo_row, halo_row, lambda s: halo_f.at[r + 1, s, my_rows])
        to_frames(4, r, lambda to: foot.at[r, :, my_rows], lambda at: foot.at[r, :, group_rows(at)])
        if not last:
            from_neighbours(1, lambda s: halo_f.at[r + 1, s, my_rows])
            for side in range(2):
                to_frames(
                    6 + side,
                    r,
                    lambda to, side=side: halo_f.at[r + 1, side, my_rows],
                    lambda at, side=side: halo_f.at[r + 1, side, group_rows(at)],
                )
        level_send(1, level_sum(0))
        from_frames(5, r, lambda at: bgs.at[r, at])
        from_frames(4, r, lambda at: foot.at[r, :, group_rows(at)])
        packed = level_sum(1)
        for c in range(2):
            change = packed[c : c + 1] / (2.0 * packed[2 + c : 3 + c])
            change = dot_nt(eye32, jnp.broadcast_to(change, (NC, FR)), HIGH)
            bts[c] = jnp.maximum(bts[c] + change, 0.0)

    out_tr[...] = dot_nt(eye, traces_now, HIGH)
    out_f[...] = foot[ROUNDS - 1]
    out_bg[...] = bgs[ROUNDS - 1]
    both = jnp.where(lanes(FR) == 0, bts[0], jnp.where(lanes(FR) == 1, bts[1], 0.0))
    out_bt[...] = dot_nt(eye[0:8], both, HIGH)[0:2]
    for copy in sends:
        copy.wait_send()


def solution(mesh):
    nsp = mesh.shape["space"]
    near = min(8, nsp)
    levels = ((1, near), (near, nsp // near))
    vmem = pl.BlockSpec(memory_space=pltpu.VMEM)
    far = pl.BlockSpec(memory_space=pltpu.HBM)
    smem = pl.BlockSpec(memory_space=pltpu.SMEM)

    def body(activity, footprints, traces, bg_space, bg_time, block_lists, group_order):
        f0 = footprints[0].reshape(NC, BPG, BV).transpose(1, 0, 2)
        tr0 = traces.reshape(NC, FR)
        out_tr, out_f, out_bg, out_bt = pl.pallas_call(
            functools.partial(kernel, nsp, levels),
            out_shape=(
                jax.ShapeDtypeStruct((NC, FR), F32),
                jax.ShapeDtypeStruct((BPG, NC, BV), BF16),
                jax.ShapeDtypeStruct((8, 16, BV), BF16),
                jax.ShapeDtypeStruct((2, FR), F32),
            ),
            in_specs=[far, vmem, far, far, far, smem, smem],
            out_specs=(vmem,) * 4,
            scratch_shapes=[
                pltpu.VMEM((VB, FR, BV), BF16),
                pltpu.VMEM((2, VB, BV), F32),
                pltpu.VMEM((NC, FR), F32),
                pltpu.VMEM((2, FR), F32),
                pltpu.VMEM((FR, BPG * NC), jnp.int32),
                pltpu.VMEM((2 * ROUNDS, EXT, FR, BV), BF16),
                pltpu.VMEM((BPG, NG * FR, BV), BF16),
                pltpu.VMEM((ROUNDS, BPG, NC, BV), BF16),
                pltpu.VMEM((ROUNDS, 8, 16, BV), BF16),
                pltpu.VMEM((2, FR, NC), F32),
                pltpu.VMEM((ROUNDS, 2, NC, BV), BF16),
                pltpu.VMEM((NC, BV), BF16),
                pltpu.VMEM((G, BV), BF16),
                pltpu.VMEM((ROUNDS + 1, 2, FR + G, NC), BF16),
                pltpu.VMEM((ROUNDS + 1, FR + G, NC), BF16),
                pltpu.VMEM((ROUNDS, 2, FR, NC), F32),
                pltpu.VMEM((ROUNDS, 2, FR, NC), F32),
                pltpu.VMEM((ROUNDS, G + 8, NC), F32),
                pltpu.VMEM((ROUNDS, NT, G + 8, NC), F32),
                pltpu.VMEM((ROUNDS, BPG - 1, NC, BV), BF16),
                pltpu.VMEM((ROUNDS, NT, BPG - 1, G, BV), BF16),
                pltpu.VMEM((ROUNDS, 8, FR, BV), BF16),
                pltpu.VMEM((NG * FR, BV), BF16),
                pltpu.VMEM((ROUNDS, NC, BV), BF16),
                pltpu.VMEM((ROUNDS, NT, G, BV), BF16),
                pltpu.VMEM((ROUNDS, NT, 16, BV), BF16),
                pltpu.VMEM((ROUNDS, NT, 16, BV), BF16),
                pltpu.VMEM((8 * FR, 48), F32),
                pltpu.VMEM((ROUNDS, 2, 8, 8, FR), F32),
                pltpu.VMEM((2, NC, NG * FR), BF16),
                pltpu.VMEM((48, 8 * FR), BF16),
                pltpu.SemaphoreType.DMA((4,)),
                pltpu.SemaphoreType.DMA((9, 2)),
                pltpu.SemaphoreType.DMA((9, 2)),
                pltpu.SemaphoreType.DMA((8, ROUNDS, NT)),
                pltpu.SemaphoreType.DMA((8, ROUNDS, NT)),
                pltpu.SemaphoreType.DMA((ROUNDS, 2, 8)),
                pltpu.SemaphoreType.DMA((ROUNDS, 2, 8)),
            ],
            compiler_params=pltpu.CompilerParams(
                collective_id=0, has_side_effects=True, vmem_limit_bytes=52 * 1024 * 1024
            ),
        )(activity, f0, tr0, bg_space, bg_time, block_lists[0].T, group_order[0])
        return (
            out_tr.reshape(1, NG, G, FR),
            out_f.transpose(1, 0, 2).reshape(1, NG, G, BPG, BV),
            out_bg.reshape(8, 2, 8, BV).transpose(1, 0, 2, 3).reshape(2, VB, BV).astype(F32),
            out_bt,
        )

    return jax.shard_map(
        body,
        mesh=mesh,
        in_specs=(
            P("space", "tm", None),
            P("space", None, None, None, None),
            P("space", None, None, "tm"),
            P(None, "space", None),
            P(None, "tm"),
            P("space", None, None),
            P("space", None),
        ),
        out_specs=(
            P("space", None, None, "tm"),
            P("space", None, None, None, None),
            P(None, "space", None),
            P(None, "tm"),
        ),
        check_vma=False,
    )
```

```python
import functools

import jax
import jax.numpy as jnp
from jax import lax
from jax.experimental import pallas as pl
from jax.experimental.pallas import tpu as pltpu
from jax.sharding import PartitionSpec as P

MESH = pl.DeviceIdType.MESH
HIGH = lax.Precision.HIGHEST
F32 = jnp.float32
BF16 = jnp.bfloat16

G = 16
NG = 8
NC = NG * G
BPG = 4
BV = 512
VB = 64
EXT = 72
FR = 32
NT = 8
ROUNDS = 2
RIDGE_TRACE = 0.01 * BPG * BV
RIDGE_FOOT = 0.1 * FR * NT


def dot(a, b, precision=None):
    return lax.dot_general(a, b, (((1,), (0,)), ((), ())), precision=precision, preferred_element_type=F32)


def dot_nt(a, b, precision=None):
    return lax.dot_general(a, b, (((1,), (1,)), ((), ())), precision=precision, preferred_element_type=F32)


def split3(x):
    hi = x.astype(BF16).astype(F32)
    rest = x - hi
    mid = rest.astype(BF16).astype(F32)
    return hi, mid, rest - mid


def halves(x):
    high = x.astype(BF16)
    return high, (x - high.astype(F32)).astype(BF16)


def lanes(rows):
    return lax.broadcasted_iota(jnp.int32, (rows, NC), 1)


def fold_diagonal(square):
    group = lanes(G) // G
    out = jnp.zeros((G, NC), F32)
    for h in range(NG):
        out = out + jnp.where(group == h, square[h * G : (h + 1) * G], 0.0)
    return out


def spread_diagonal(folded):
    group = lanes(G) // G
    return jnp.concatenate([jnp.where(group == h, folded, 0.0) for h in range(NG)], axis=0)


def inverse_blocks(folded, ridge):
    first = lanes(G) % G
    sub = lax.broadcasted_iota(jnp.int32, (G, NC), 0)
    folded = folded + jnp.where(sub == first, ridge, 0.0)
    rows = []
    for n in range(G):
        moved = folded if n == 0 else pltpu.roll(folded, NC - n, 1)
        rows.append(jnp.where(first == 0, moved, jnp.where(sub == n, 1.0, 0.0)))
    for p in range(G):
        pivot = 1.0 / rows[p][p : p + 1]
        at = sub == p
        scaled = jnp.where(at, jnp.broadcast_to(pivot, (G, NC)), rows[p] * pivot)
        for n in range(G):
            if n != p:
                rows[n] = jnp.where(at, 0.0, rows[n]) - rows[n][p : p + 1] * scaled
        rows[p] = scaled
    out = jnp.zeros((G, NC), F32)
    for n in range(G):
        moved = rows[n] if n == 0 else pltpu.roll(rows[n], n, 1)
        out = jnp.where(first == n, moved, out)
    return spread_diagonal(out)


def kernel(
    nsp, levels,
    act_hbm, f0, small, bg_hbm, bl,
    out_tr, out_f, out_bg, out_bt,
    act, bg0, blrow, res, pieces, foot, bgs, bts, halo_f, halo_out, halo_row, tl_in, tl_out, dr_out, dr_in, corr_out, corr_in,
    part_out, part_in, edge_in, edge_pieces, edge_out, edge_sum, frame_out, frame_in, vacc, vox, zs, btm,
    in_sem, nb_s, nb_r, tm_s, tm_r, vx_s, vx_r,
):
    loads = [
        pltpu.make_async_copy(there, here, in_sem.at[i])
        for i, (there, here) in enumerate(
            ((bg_hbm, bg0), (act_hbm, act))
        )
    ]
    for load in loads:
        load.start()
    me = lax.axis_index("tm")
    sp = lax.axis_index("space")
    left = lax.rem(sp + nsp - 1, nsp)
    right = lax.rem(sp + 1, nsp)
    peers = []
    for stride, size in levels:
        q = lax.rem(sp // stride, size)
        row = []
        for d in range(1, size):
            other = lax.rem(q + d, size)
            row.append((sp + (other - q) * stride, other))
        peers.append((q, row))

    barrier = pltpu.get_barrier_semaphore()
    count = 0
    for d in range(1, NT):
        pl.semaphore_signal(barrier, inc=1, device_id=(sp, lax.rem(me + d, NT)), device_id_type=MESH)
        count += 1
    for other in (left, right):
        pl.semaphore_signal(barrier, inc=1, device_id=(other, me), device_id_type=MESH)
        count += 1
    for _, row in peers:
        for other, _ in row:
            pl.semaphore_signal(barrier, inc=1, device_id=(other, me), device_id_type=MESH)
            count += 1

    sends = []

    def send(src, dst, ssem, rsem, device):
        copy = pltpu.make_async_remote_copy(
            src_ref=src, dst_ref=dst, send_sem=ssem, recv_sem=rsem, device_id=device, device_id_type=MESH
        )
        copy.start()
        sends.append(copy)

    def arrived(ref, ssem, rsem, device):
        pltpu.make_async_remote_copy(
            src_ref=ref, dst_ref=ref, send_sem=ssem, recv_sem=rsem, device_id=device, device_id_type=MESH
        ).wait_recv()

    def to_neighbours(cat, src_left, src_right, dst):
        send(src_right, dst(0), nb_s.at[cat, 0], nb_r.at[cat, 0], (right, me))
        send(src_left, dst(1), nb_s.at[cat, 1], nb_r.at[cat, 1], (left, me))

    def from_neighbours(cat, dst):
        arrived(dst(0), nb_s.at[cat, 0], nb_r.at[cat, 0], (left, me))
        arrived(dst(1), nb_s.at[cat, 1], nb_r.at[cat, 1], (right, me))

    def to_frames(kind, r, src, dst):
        for d in range(1, NT):
            to = lax.rem(me + d, NT)
            send(src(to), dst(me), tm_s.at[kind, r, to], tm_r.at[kind, r, me], (sp, to))

    def from_frames(kind, r, dst):
        for d in range(1, NT):
            other = lax.rem(me + d, NT)
            arrived(dst(other), tm_s.at[kind, r, other], tm_r.at[kind, r, other], (sp, other))

    def group_rows(i):
        return pl.ds(pl.multiple_of(i * G, G), G)

    entry = [[bl[k, g] for k in range(BPG)] for g in range(NG)]
    group32 = lanes(FR) // G

    for k in range(BPG):
        row = jnp.zeros((FR, NC), jnp.int32)
        for g in range(NG):
            row = jnp.where(group32 == g, entry[g][k], row)
        blrow[:, k * NC : (k + 1) * NC] = row
    halo_id = jnp.full((G, NC), -1, jnp.int32)
    halo_k, halo_any, halo_at = [], [], []
    group16 = lanes(G) // G
    for g in range(NG):
        hid = jnp.int32(-1)
        hk = jnp.int32(0)
        for k in range(BPG):
            out = jnp.logical_or(entry[g][k] < 4, entry[g][k] >= 68)
            hid = jnp.where(out, entry[g][k], hid)
            hk = jnp.where(out, k, hk)
        halo_id = jnp.where(group16 == g, hid, halo_id)
        halo_k.append(hk)
        halo_any.append(hid >= 0)
        halo_at.append(jnp.where(hid >= 68, hid - 64, jnp.maximum(hid, 0)))
    halo_bf = halo_id.astype(F32).astype(BF16)

    def stage_traces(i, low):
        tl_out[i, 0:FR, :] = low
        tl_out[i, FR : FR + G, :] = halo_bf

    def gram_of(source):
        everything = source[...].reshape(BPG * NC, BV)
        total = jnp.zeros((NC, NC), F32)
        for k in range(BPG):
            product = dot_nt(source[k], everything)
            column = jnp.concatenate([jnp.full((G, NC), entry[g][k], jnp.int32) for g in range(NG)], axis=0)
            for j in range(BPG):
                row = blrow[:, j * NC : (j + 1) * NC]
                row = jnp.concatenate([row] * (NC // FR), axis=0)
                total = total + jnp.where(column == row, product[:, j * NC : (j + 1) * NC], 0.0)
        return total

    def field(r, j):
        if r == 0:
            rows = pl.ds(pl.multiple_of(8 * j, 8), 8)
            return jnp.concatenate([bg0[0, rows, :], bg0[1, rows, :]], axis=0)
        return bgs[r - 1, j].astype(F32)

    def chunk(inst, j, source, low4, traces_i, r, side, drive):
        parts = []
        for i in range(8):
            parts.append(jnp.where(blrow[...] == 8 * j + 4 + i, low4, 0.0).astype(BF16))
        lhs = jnp.concatenate(parts, axis=0)
        rebuilt = dot(lhs, source[...].reshape(BPG * NC, BV))
        if side is not None:
            low = tl_in[traces_i, side, 0:FR, :].astype(F32)
            hid = tl_in[traces_i, side, FR : FR + G, :].astype(F32)
            hid = jnp.concatenate([hid, hid], axis=0)
            base = 68.0 if side == 0 else 0.0
            near = jnp.concatenate(
                [jnp.where(hid == base + i, low, 0.0).astype(BF16) for i in range(4)], axis=0
            )
            near = dot(near, halo_f[r, side])
            edge = slice(0, 4) if side == 0 else slice(4, 8)
            if side == 0:
                rebuilt = jnp.concatenate([rebuilt[: 4 * FR] + near, rebuilt[4 * FR :]], axis=0)
            else:
                rebuilt = jnp.concatenate([rebuilt[: 4 * FR], rebuilt[4 * FR :] + near], axis=0)
        t0 = jnp.concatenate([bts[0]] * (BV // NC), axis=1)
        t1 = jnp.concatenate([bts[1]] * (BV // NC), axis=1)
        s = field(r, j)
        s0, s1 = s[0:8], s[8:16]
        out = []
        for i in range(8):
            backdrop = s0[i : i + 1] * t0 + s1[i : i + 1] * t1
            seen = act[8 * j + i].astype(F32)
            value = ((seen - rebuilt[i * FR : (i + 1) * FR]) - backdrop).astype(BF16)
            res[inst, 8 * j + 4 + i] = value
            out.append(value)
        if side is not None and drive:
            flat = jnp.concatenate(out[edge], axis=0)
            back = dot_nt(flat, halo_f[r, side])
            total = jnp.zeros((FR, NC), F32)
            for i in range(4):
                total = total + jnp.where(hid == base + i, back[i * FR : (i + 1) * FR], 0.0)
            dr_out[r, side] = total

    def background(inst, r):
        def body(j, carry):
            flat = res[inst, pl.ds(8 * j + 4, 8)].reshape(8 * FR, BV)
            frame = dot(btm[...], flat)
            frame_out[r, j] = (frame[0:16] + frame[16:32] + frame[32:48]).astype(BF16)
            s = jnp.concatenate([x.astype(BF16) for x in split3(field(r, j))], axis=0)
            vacc[...] += dot_nt(flat, s)
            return carry

        lax.fori_loop(0, 8, body, 0)

    def middle(inst, source, low4, r, start, stop):
        def body(j, carry):
            chunk(inst, j, source, low4, None, r, None, False)
            return carry

        lax.fori_loop(start, stop, body, 0)

    def edges(inst, source, low4, traces_i, r, drive):
        chunk(inst, 0, source, low4, traces_i, r, 0, drive)
        chunk(inst, 7, source, low4, traces_i, r, 1, drive)

    def four(low):
        return jnp.concatenate([low.astype(F32)] * BPG, axis=1)

    def gather(inst):
        for g in range(NG):
            for k in range(BPG):
                pieces[k, g * FR : (g + 1) * FR, :] = res[inst, entry[g][k]]

    eye32 = jnp.where(
        lax.broadcasted_iota(jnp.int32, (FR, FR), 0) == lax.broadcasted_iota(jnp.int32, (FR, FR), 1), 1.0, 0.0
    )
    eye = jnp.where(lax.broadcasted_iota(jnp.int32, (NC, NC), 0) == lanes(NC), 1.0, 0.0)
    traces_now = dot_nt(eye32, small[0:NC, :], HIGH)
    for c in range(2):
        bts[c] = dot_nt(eye32, jnp.broadcast_to(small[NC + c : NC + c + 1, :], (NC, FR)), HIGH)
    low = traces_now.astype(BF16)
    for g in range(NG):
        halo_out[g * G : (g + 1) * G, :] = f0[halo_k[g], g * G : (g + 1) * G, :]
    stage_traces(0, low)
    for i in range(2 * ROUNDS):
        res[i, 0:4] = jnp.zeros((4, FR, BV), BF16)
        res[i, 68:72] = jnp.zeros((4, FR, BV), BF16)

    pl.semaphore_wait(barrier, count)
    to_neighbours(0, halo_out, halo_out, lambda s: halo_f.at[0, s])
    to_neighbours(2, tl_out.at[0], tl_out.at[0], lambda s: tl_in.at[0, s])

    for r in range(ROUNDS):
        source = f0 if r == 0 else foot.at[0]
        def first_edges():
            if r == 0:
                from_neighbours(0, lambda s: halo_f.at[0, s])
                from_neighbours(2, lambda s: tl_in.at[0, s])
            else:
                for side in range(2):
                    from_frames(6 + side, r - 1, lambda at, side=side: halo_f.at[r, side, group_rows(at)])
            edges(2 * r, source, four(low), r, r, True)
            to_neighbours(5 + 2 * r, dr_out.at[r, 0], dr_out.at[r, 1], lambda s: dr_in.at[r, s])

        if r > 0:
            first_edges()
        gram = gram_of(source)
        inverse = inverse_blocks(fold_diagonal(gram), RIDGE_TRACE)
        weights = dot(gram, inverse, HIGH)

        if r == 0:
            loads[0].wait()
            loads[1].wait()
        middle(2 * r, source, four(low), r, 1, 7)
        if r == 0:
            first_edges()
        gather(2 * r)
        cross = jnp.zeros((NG * FR, NC), F32)
        for k in range(BPG):
            cross = cross + dot_nt(pieces[k], source[k])
        drives = jnp.zeros((FR, NC), F32)
        for g in range(NG):
            drives = drives + jnp.where(group32 == g, cross[g * FR : (g + 1) * FR], 0.0)
        from_neighbours(5 + 2 * r, lambda s: dr_in.at[r, s])
        drives = drives + (dr_in[r, 0] + dr_in[r, 1])
        drives = dot(drives, inverse, HIGH)
        high, rest = halves(weights)
        weights = jnp.concatenate([high, high, rest], axis=0)
        current = traces_now
        for p in range(NG):
            high, rest = halves(current - traces_now)
            coupled = dot(jnp.concatenate([high, rest, high], axis=1), weights)
            fresh = jnp.maximum(current + (drives - coupled), 0.0)
            current = jnp.where(group32 == bl[BPG, p], fresh, current)
        traces_now = current
        low = traces_now.astype(BF16)

        stage_traces(r + 1, low)
        to_neighbours(3 + r, tl_out.at[r + 1], tl_out.at[r + 1], lambda s: tl_in.at[r + 1, s])
        corr = lax.dot_general(
            traces_now, traces_now, (((0,), (0,)), ((), ())), precision=HIGH, preferred_element_type=F32
        )
        sq = [jnp.sum(bts[c] * bts[c], axis=0, keepdims=True) for c in range(2)]
        corr_out[r, 0:G, :] = fold_diagonal(corr)
        corr_out[r, G : G + 4, :] = jnp.broadcast_to(sq[0], (4, NC))
        corr_out[r, G + 4 : G + 8, :] = jnp.broadcast_to(sq[1], (4, NC))
        to_frames(0, r, lambda to: corr_out.at[r], lambda at: corr_in.at[r, at])

        inst = 2 * r + 1
        middle(inst, source, four(low), r, 1, 7)
        lane = lanes(FR)
        spread = jnp.zeros((FR, NC), F32)
        for c in range(2):
            for s, part in enumerate(split3(bts[c])):
                spread = jnp.where(lane // 8 == s * 2 + c, part, spread)
        stacked = jnp.concatenate(
            [jnp.where(lane % 8 == b, spread, 0.0).astype(BF16) for b in range(8)], axis=0
        )
        btm[...] = dot_nt(eye[0:48].astype(BF16), stacked).astype(BF16)
        vacc[...] = jnp.zeros_like(vacc)

        from_neighbours(3 + r, lambda s: tl_in.at[r + 1, s])
        edges(inst, source, four(low), r + 1, r, False)
        cat = 5 + inst
        to_neighbours(
            cat, res.at[inst, pl.ds(4, 4)], res.at[inst, pl.ds(64, 4)], lambda s: edge_in.at[r, pl.ds(4 * s, 4)]
        )

        from_frames(0, r, lambda at: corr_in.at[r, at])
        corr_in[r, me] = corr_out[r]
        total = corr_in[r, 0]
        for s in range(1, NT):
            total = total + corr_in[r, s]
        inverse_a = inverse_blocks(total[0:G], RIDGE_FOOT)
        square_time = [total[G : G + 1], total[G + 4 : G + 5]]
        masked = jnp.concatenate(
            [jnp.where(group32 == g, low.astype(F32), 0.0) for g in range(NG)], axis=0
        )
        z = dot_nt(inverse_a, masked, HIGH)
        z_high = z.astype(BF16)
        zs[0] = z_high
        zs[1] = (z - z_high.astype(F32)).astype(BF16)

        for g in range(NG):
            for k in range(BPG - 1):
                at = jnp.where(halo_k[g] <= k, entry[g][k + 1], entry[g][k])
                pieces[k, g * FR : (g + 1) * FR, :] = res[inst, at]
        for k in range(BPG - 1):
            part_out[r, k] = (dot(zs[0], pieces[k]) + dot(zs[1], pieces[k])).astype(BF16)
        to_frames(1, r, lambda to: part_out.at[r, :, group_rows(to)], lambda at: part_in.at[r, at])

        background(inst, r)
        to_frames(3, r, lambda to: frame_out.at[r, to], lambda at: frame_in.at[r, at])

        from_neighbours(cat, lambda s: edge_in.at[r, pl.ds(4 * s, 4)])
        for g in range(NG):
            block = edge_in[r, halo_at[g]]
            own = res[inst, jnp.where(halo_any[g], 4, entry[g][0])]
            edge_pieces[g * FR : (g + 1) * FR, :] = jnp.where(
                halo_any[g], block.astype(F32), own.astype(F32)
            ).astype(BF16)
        edge_out[r] = (dot(zs[0], edge_pieces[...]) + dot(zs[1], edge_pieces[...])).astype(BF16)
        to_frames(2, r, lambda to: edge_out.at[r, group_rows(to)], lambda at: edge_sum.at[r, at])

        row = lax.broadcasted_iota(jnp.int32, (FR, 48), 0)
        col = lax.broadcasted_iota(jnp.int32, (FR, 48), 1)
        summed = jnp.zeros((FR, 48), F32)
        for b in range(8):
            summed = summed + jnp.where(col % 8 == b, vacc[b * FR : (b + 1) * FR, :], 0.0)
        packed = jnp.zeros((FR, NC), F32)
        for c in range(2):
            total = jnp.sum(jnp.where((col // 8) % 2 == c, summed, 0.0), axis=1, keepdims=True)
            packed = jnp.where(lane == c, total, packed)
            squares = jnp.zeros((8, BV), F32)
            for j in range(8):
                part = field(r, j)[c * 8 : (c + 1) * 8]
                squares = squares + part * part
            squares = jnp.sum(jnp.sum(squares, axis=0, keepdims=True), axis=1, keepdims=True)
            packed = jnp.where(lane == 2 + c, squares, packed)

        def level_send(i, value):
            q, rows = peers[i]
            vox[r, i, q] = value
            for other, oq in rows:
                send(vox.at[r, i, q], vox.at[r, i, q], vx_s.at[r, i, oq], vx_r.at[r, i, q], (other, me))

        def level_sum(i):
            q, rows = peers[i]
            for other, oq in rows:
                arrived(vox.at[r, i, oq], vx_s.at[r, i, oq], vx_r.at[r, i, oq], (other, me))
            total = vox[r, i, 0]
            for s in range(1, levels[i][1]):
                total = total + vox[r, i, s]
            return total

        level_send(0, dot_nt(eye[0:8], packed, HIGH))

        frame = frame_out[r, me].astype(F32)
        from_frames(3, r, lambda at: frame_in.at[r, at])
        for d in range(1, NT):
            frame = frame + frame_in[r, lax.rem(me + d, NT)].astype(F32)
        scale = jnp.concatenate([jnp.broadcast_to(square_time[c], (8, NC)) for c in range(2)], axis=0)
        scale = jnp.concatenate([scale] * (BV // NC), axis=1)
        bgs[r, me] = jnp.maximum(field(r, me) + frame / (2.0 * scale), 0.0).astype(BF16)
        to_frames(5, r, lambda to: bgs.at[r, me], lambda at: bgs.at[r, at])
        my_rows = group_rows(me)
        total = part_out[r, :, my_rows].astype(F32)
        from_frames(1, r, lambda at: part_in.at[r, at])
        for d in range(1, NT):
            total = total + part_in[r, lax.rem(me + d, NT)].astype(F32)
        from_frames(2, r, lambda at: edge_sum.at[r, at])
        extra = edge_out[r, my_rows].astype(F32)
        for d in range(1, NT):
            extra = extra + edge_sum[r, lax.rem(me + d, NT)].astype(F32)
        which = jnp.int32(0)
        for k in range(BPG):
            mine = bl[k, me]
            which = jnp.where(jnp.logical_or(mine < 4, mine >= 68), k, which)
        for k in range(BPG):
            moved = jnp.where(which < k, total[max(k - 1, 0)], total[min(k, BPG - 2)])
            moved = jnp.where(which == k, extra, moved)
            fresh = jnp.maximum(source[k, my_rows, :].astype(F32) + moved, 0.0)
            foot[r, k, my_rows, :] = fresh.astype(BF16)
            spill = fresh if k == 0 else jnp.where(which == k, fresh, spill)
        last = r + 1 == ROUNDS
        if not last:
            halo_row[...] = spill.astype(BF16)
            to_neighbours(1, halo_row, halo_row, lambda s: halo_f.at[r + 1, s, my_rows])
        to_frames(4, r, lambda to: foot.at[r, :, my_rows], lambda at: foot.at[r, :, group_rows(at)])
        if not last:
            from_neighbours(1, lambda s: halo_f.at[r + 1, s, my_rows])
            for side in range(2):
                to_frames(
                    6 + side,
                    r,
                    lambda to, side=side: halo_f.at[r + 1, side, my_rows],
                    lambda at, side=side: halo_f.at[r + 1, side, group_rows(at)],
                )
        level_send(1, level_sum(0))
        from_frames(5, r, lambda at: bgs.at[r, at])
        from_frames(4, r, lambda at: foot.at[r, :, group_rows(at)])
        packed = level_sum(1)
        for c in range(2):
            change = packed[c : c + 1] / (2.0 * packed[2 + c : 3 + c])
            change = dot_nt(eye32, jnp.broadcast_to(change, (NC, FR)), HIGH)
            bts[c] = jnp.maximum(bts[c] + change, 0.0)

    out_tr[...] = dot_nt(eye, traces_now, HIGH)
    out_f[...] = foot[ROUNDS - 1]
    out_bg[...] = bgs[ROUNDS - 1]
    both = jnp.where(lanes(FR) == 0, bts[0], jnp.where(lanes(FR) == 1, bts[1], 0.0))
    out_bt[...] = dot_nt(eye[0:8], both, HIGH)[0:2]
    for copy in sends:
        copy.wait_send()


def solution(mesh):
    nsp = mesh.shape["space"]
    near = min(8, nsp)
    levels = ((1, near), (near, nsp // near))
    vmem = pl.BlockSpec(memory_space=pltpu.VMEM)
    far = pl.BlockSpec(memory_space=pltpu.HBM)
    smem = pl.BlockSpec(memory_space=pltpu.SMEM)

    def body(activity, footprints, traces, bg_space, bg_time, block_lists, group_order):
        f0 = footprints[0].reshape(NC, BPG, BV).transpose(1, 0, 2)
        small = jnp.concatenate([traces.reshape(NC, FR), bg_time], axis=0)
        lists = jnp.concatenate([block_lists[0].T, group_order], axis=0)
        out_tr, out_f, out_bg, out_bt = pl.pallas_call(
            functools.partial(kernel, nsp, levels),
            out_shape=(
                jax.ShapeDtypeStruct((NC, FR), F32),
                jax.ShapeDtypeStruct((BPG, NC, BV), BF16),
                jax.ShapeDtypeStruct((8, 16, BV), BF16),
                jax.ShapeDtypeStruct((2, FR), F32),
            ),
            in_specs=[far, vmem, vmem, far, smem],
            out_specs=(vmem,) * 4,
            scratch_shapes=[
                pltpu.VMEM((VB, FR, BV), BF16),
                pltpu.VMEM((2, VB, BV), F32),
                pltpu.VMEM((FR, BPG * NC), jnp.int32),
                pltpu.VMEM((2 * ROUNDS, EXT, FR, BV), BF16),
                pltpu.VMEM((BPG, NG * FR, BV), BF16),
                pltpu.VMEM((ROUNDS, BPG, NC, BV), BF16),
                pltpu.VMEM((ROUNDS, 8, 16, BV), BF16),
                pltpu.VMEM((2, FR, NC), F32),
                pltpu.VMEM((ROUNDS, 2, NC, BV), BF16),
                pltpu.VMEM((NC, BV), BF16),
                pltpu.VMEM((G, BV), BF16),
                pltpu.VMEM((ROUNDS + 1, 2, FR + G, NC), BF16),
                pltpu.VMEM((ROUNDS + 1, FR + G, NC), BF16),
                pltpu.VMEM((ROUNDS, 2, FR, NC), F32),
                pltpu.VMEM((ROUNDS, 2, FR, NC), F32),
                pltpu.VMEM((ROUNDS, G + 8, NC), F32),
                pltpu.VMEM((ROUNDS, NT, G + 8, NC), F32),
                pltpu.VMEM((ROUNDS, BPG - 1, NC, BV), BF16),
                pltpu.VMEM((ROUNDS, NT, BPG - 1, G, BV), BF16),
                pltpu.VMEM((ROUNDS, 8, FR, BV), BF16),
                pltpu.VMEM((NG * FR, BV), BF16),
                pltpu.VMEM((ROUNDS, NC, BV), BF16),
                pltpu.VMEM((ROUNDS, NT, G, BV), BF16),
                pltpu.VMEM((ROUNDS, NT, 16, BV), BF16),
                pltpu.VMEM((ROUNDS, NT, 16, BV), BF16),
                pltpu.VMEM((8 * FR, 48), F32),
                pltpu.VMEM((ROUNDS, 2, 8, 8, FR), F32),
                pltpu.VMEM((2, NC, NG * FR), BF16),
                pltpu.VMEM((48, 8 * FR), BF16),
                pltpu.SemaphoreType.DMA((2,)),
                pltpu.SemaphoreType.DMA((9, 2)),
                pltpu.SemaphoreType.DMA((9, 2)),
                pltpu.SemaphoreType.DMA((8, ROUNDS, NT)),
                pltpu.SemaphoreType.DMA((8, ROUNDS, NT)),
                pltpu.SemaphoreType.DMA((ROUNDS, 2, 8)),
                pltpu.SemaphoreType.DMA((ROUNDS, 2, 8)),
            ],
            compiler_params=pltpu.CompilerParams(
                collective_id=0, has_side_effects=True, vmem_limit_bytes=52 * 1024 * 1024
            ),
        )(activity, f0, small, bg_space, lists)
        return (
            out_tr.reshape(1, NG, G, FR),
            out_f.transpose(1, 0, 2).reshape(1, NG, G, BPG, BV),
            out_bg.reshape(8, 2, 8, BV).transpose(1, 0, 2, 3).reshape(2, VB, BV).astype(F32),
            out_bt,
        )

    return jax.shard_map(
        body,
        mesh=mesh,
        in_specs=(
            P("space", "tm", None),
            P("space", None, None, None, None),
            P("space", None, None, "tm"),
            P(None, "space", None),
            P(None, "tm"),
            P("space", None, None),
            P("space", None),
        ),
        out_specs=(
            P("space", None, None, "tm"),
            P("space", None, None, None, None),
            P(None, "space", None),
            P(None, "tm"),
        ),
        check_vma=False,
    )
```

```python
import functools

import jax
import jax.numpy as jnp
from jax import lax
from jax.experimental import pallas as pl
from jax.experimental.pallas import tpu as pltpu
from jax.sharding import PartitionSpec as P

MESH = pl.DeviceIdType.MESH
HIGH = lax.Precision.HIGHEST
F32 = jnp.float32
BF16 = jnp.bfloat16

G = 16
NG = 8
NC = NG * G
BPG = 4
BV = 512
VB = 64
EXT = 72
FR = 32
NT = 8
ROUNDS = 2
RIDGE_TRACE = 0.01 * BPG * BV
RIDGE_FOOT = 0.1 * FR * NT


def dot(a, b, precision=None):
    return lax.dot_general(a, b, (((1,), (0,)), ((), ())), precision=precision, preferred_element_type=F32)


def dot_nt(a, b, precision=None):
    return lax.dot_general(a, b, (((1,), (1,)), ((), ())), precision=precision, preferred_element_type=F32)


def split3(x):
    hi = x.astype(BF16).astype(F32)
    rest = x - hi
    mid = rest.astype(BF16).astype(F32)
    return hi, mid, rest - mid


def halves(x):
    high = x.astype(BF16)
    return high, (x - high.astype(F32)).astype(BF16)


def lanes(rows):
    return lax.broadcasted_iota(jnp.int32, (rows, NC), 1)


def fold_diagonal(square):
    group = lanes(G) // G
    out = jnp.zeros((G, NC), F32)
    for h in range(NG):
        out = out + jnp.where(group == h, square[h * G : (h + 1) * G], 0.0)
    return out


def spread_diagonal(folded):
    group = lanes(G) // G
    return jnp.concatenate([jnp.where(group == h, folded, 0.0) for h in range(NG)], axis=0)


def inverse_blocks(folded, ridge):
    first = lanes(G) % G
    sub = lax.broadcasted_iota(jnp.int32, (G, NC), 0)
    folded = folded + jnp.where(sub == first, ridge, 0.0)
    rows = []
    for n in range(G):
        moved = folded if n == 0 else pltpu.roll(folded, NC - n, 1)
        rows.append(jnp.where(first == 0, moved, jnp.where(sub == n, 1.0, 0.0)))
    for p in range(G):
        pivot = 1.0 / rows[p][p : p + 1]
        at = sub == p
        scaled = jnp.where(at, jnp.broadcast_to(pivot, (G, NC)), rows[p] * pivot)
        for n in range(G):
            if n != p:
                rows[n] = jnp.where(at, 0.0, rows[n]) - rows[n][p : p + 1] * scaled
        rows[p] = scaled
    out = jnp.zeros((G, NC), F32)
    for n in range(G):
        moved = rows[n] if n == 0 else pltpu.roll(rows[n], n, 1)
        out = jnp.where(first == n, moved, out)
    return spread_diagonal(out)


def kernel(
    nsp, levels,
    act_hbm, f0, small, bg_hbm, bl,
    out_tr, out_f, out_bg, out_bt,
    act, bg0, blrow, res, pieces, foot, bgs, bts, halo_f, halo_out, halo_row, tl_in, tl_out, dr_out, dr_in, corr_out, corr_in,
    part_out, part_in, edge_in, edge_pieces, edge_out, edge_sum, frame_out, frame_in, vacc, vox, zs, btm,
    in_sem, nb_s, nb_r, tm_s, tm_r, vx_s, vx_r,
):
    loads = [
        pltpu.make_async_copy(there, here, in_sem.at[i])
        for i, (there, here) in enumerate(
            ((bg_hbm, bg0), (act_hbm, act))
        )
    ]
    for load in loads:
        load.start()
    me = lax.axis_index("tm")
    sp = lax.axis_index("space")
    left = lax.rem(sp + nsp - 1, nsp)
    right = lax.rem(sp + 1, nsp)
    peers = []
    for stride, size in levels:
        q = lax.rem(sp // stride, size)
        row = []
        for d in range(1, size):
            other = lax.rem(q + d, size)
            row.append((sp + (other - q) * stride, other))
        peers.append((q, row))

    barrier = pltpu.get_barrier_semaphore()
    count = 0
    for d in range(1, NT):
        pl.semaphore_signal(barrier, inc=1, device_id=(sp, lax.rem(me + d, NT)), device_id_type=MESH)
        count += 1
    for other in (left, right):
        pl.semaphore_signal(barrier, inc=1, device_id=(other, me), device_id_type=MESH)
        count += 1
    for _, row in peers:
        for other, _ in row:
            pl.semaphore_signal(barrier, inc=1, device_id=(other, me), device_id_type=MESH)
            count += 1

    sends = []

    def send(src, dst, ssem, rsem, device):
        copy = pltpu.make_async_remote_copy(
            src_ref=src, dst_ref=dst, send_sem=ssem, recv_sem=rsem, device_id=device, device_id_type=MESH
        )
        copy.start()
        sends.append(copy)

    def arrived(ref, ssem, rsem, device):
        pltpu.make_async_remote_copy(
            src_ref=ref, dst_ref=ref, send_sem=ssem, recv_sem=rsem, device_id=device, device_id_type=MESH
        ).wait_recv()

    def to_neighbours(cat, src_left, src_right, dst):
        send(src_right, dst(0), nb_s.at[cat, 0], nb_r.at[cat, 0], (right, me))
        send(src_left, dst(1), nb_s.at[cat, 1], nb_r.at[cat, 1], (left, me))

    def from_neighbours(cat, dst):
        arrived(dst(0), nb_s.at[cat, 0], nb_r.at[cat, 0], (left, me))
        arrived(dst(1), nb_s.at[cat, 1], nb_r.at[cat, 1], (right, me))

    def to_frames(kind, r, src, dst):
        for d in range(1, NT):
            to = lax.rem(me + d, NT)
            send(src(to), dst(me), tm_s.at[kind, r, to], tm_r.at[kind, r, me], (sp, to))

    def from_frames(kind, r, dst):
        for d in range(1, NT):
            other = lax.rem(me + d, NT)
            arrived(dst(other), tm_s.at[kind, r, other], tm_r.at[kind, r, other], (sp, other))

    def group_rows(i):
        return pl.ds(pl.multiple_of(i * G, G), G)

    entry = [[bl[k, g] for k in range(BPG)] for g in range(NG)]
    group32 = lanes(FR) // G

    for k in range(BPG):
        row = jnp.zeros((FR, NC), jnp.int32)
        for g in range(NG):
            row = jnp.where(group32 == g, entry[g][k], row)
        blrow[:, k * NC : (k + 1) * NC] = row
    halo_id = jnp.full((G, NC), -1, jnp.int32)
    halo_k, halo_any, halo_at = [], [], []
    group16 = lanes(G) // G
    for g in range(NG):
        hid = jnp.int32(-1)
        hk = jnp.int32(0)
        for k in range(BPG):
            out = jnp.logical_or(entry[g][k] < 4, entry[g][k] >= 68)
            hid = jnp.where(out, entry[g][k], hid)
            hk = jnp.where(out, k, hk)
        halo_id = jnp.where(group16 == g, hid, halo_id)
        halo_k.append(hk)
        halo_any.append(hid >= 0)
        halo_at.append(jnp.where(hid >= 68, hid - 64, jnp.maximum(hid, 0)))
    halo_bf = halo_id.astype(F32).astype(BF16)

    def stage_traces(i, low):
        tl_out[i, 0:FR, :] = low
        tl_out[i, FR : FR + G, :] = halo_bf

    def gram_of(source):
        everything = source[...].reshape(BPG * NC, BV)
        total = jnp.zeros((NC, NC), F32)
        for k in range(BPG):
            product = dot_nt(source[k], everything)
            column = jnp.concatenate([jnp.full((G, NC), entry[g][k], jnp.int32) for g in range(NG)], axis=0)
            for j in range(BPG):
                row = blrow[:, j * NC : (j + 1) * NC]
                row = jnp.concatenate([row] * (NC // FR), axis=0)
                total = total + jnp.where(column == row, product[:, j * NC : (j + 1) * NC], 0.0)
        return total

    def field(r, j):
        if r == 0:
            rows = pl.ds(pl.multiple_of(8 * j, 8), 8)
            return jnp.concatenate([bg0[0, rows, :], bg0[1, rows, :]], axis=0)
        return bgs[r - 1, j].astype(F32)

    def chunk(inst, j, source, low4, traces_i, r, side, drive):
        parts = []
        for i in range(8):
            parts.append(jnp.where(blrow[...] == 8 * j + 4 + i, low4, 0.0).astype(BF16))
        lhs = jnp.concatenate(parts, axis=0)
        rebuilt = dot(lhs, source[...].reshape(BPG * NC, BV))
        if side is not None:
            low = tl_in[traces_i, side, 0:FR, :].astype(F32)
            hid = tl_in[traces_i, side, FR : FR + G, :].astype(F32)
            hid = jnp.concatenate([hid, hid], axis=0)
            base = 68.0 if side == 0 else 0.0
            near = jnp.concatenate(
                [jnp.where(hid == base + i, low, 0.0).astype(BF16) for i in range(4)], axis=0
            )
            near = dot(near, halo_f[r, side])
            edge = slice(0, 4) if side == 0 else slice(4, 8)
            if side == 0:
                rebuilt = jnp.concatenate([rebuilt[: 4 * FR] + near, rebuilt[4 * FR :]], axis=0)
            else:
                rebuilt = jnp.concatenate([rebuilt[: 4 * FR], rebuilt[4 * FR :] + near], axis=0)
        t0 = jnp.concatenate([bts[0]] * (BV // NC), axis=1)
        t1 = jnp.concatenate([bts[1]] * (BV // NC), axis=1)
        s = field(r, j)
        s0, s1 = s[0:8], s[8:16]
        out = []
        for i in range(8):
            backdrop = s0[i : i + 1] * t0 + s1[i : i + 1] * t1
            seen = act[8 * j + i].astype(F32)
            value = ((seen - rebuilt[i * FR : (i + 1) * FR]) - backdrop).astype(BF16)
            res[inst, 8 * j + 4 + i] = value
            out.append(value)
        if side is not None and drive:
            flat = jnp.concatenate(out[edge], axis=0)
            back = dot_nt(flat, halo_f[r, side])
            total = jnp.zeros((FR, NC), F32)
            for i in range(4):
                total = total + jnp.where(hid == base + i, back[i * FR : (i + 1) * FR], 0.0)
            dr_out[r, side] = total

    def background(inst, r):
        def body(j, carry):
            flat = res[inst, pl.ds(8 * j + 4, 8)].reshape(8 * FR, BV)
            frame = dot(btm[...], flat)
            frame_out[r, j] = (frame[0:16] + frame[16:32] + frame[32:48]).astype(BF16)
            s = jnp.concatenate([x.astype(BF16) for x in split3(field(r, j))], axis=0)
            vacc[...] += dot_nt(flat, s)
            return carry

        lax.fori_loop(0, 8, body, 0)

    def middle(inst, source, low4, r, start, stop):
        def body(j, carry):
            chunk(inst, j, source, low4, None, r, None, False)
            return carry

        lax.fori_loop(start, stop, body, 0)

    def edges(inst, source, low4, traces_i, r, drive):
        chunk(inst, 0, source, low4, traces_i, r, 0, drive)
        chunk(inst, 7, source, low4, traces_i, r, 1, drive)

    def four(low):
        return jnp.concatenate([low.astype(F32)] * BPG, axis=1)

    def gather(inst):
        for g in range(NG):
            for k in range(BPG):
                pieces[k, g * FR : (g + 1) * FR, :] = res[inst, entry[g][k]]

    eye32 = jnp.where(
        lax.broadcasted_iota(jnp.int32, (FR, FR), 0) == lax.broadcasted_iota(jnp.int32, (FR, FR), 1), 1.0, 0.0
    )
    eye = jnp.where(lax.broadcasted_iota(jnp.int32, (NC, NC), 0) == lanes(NC), 1.0, 0.0)
    traces_now = dot_nt(eye32, small[0:NC, :], HIGH)
    for c in range(2):
        bts[c] = dot_nt(eye32, jnp.broadcast_to(small[NC + c : NC + c + 1, :], (NC, FR)), HIGH)
    low = traces_now.astype(BF16)
    for g in range(NG):
        halo_out[g * G : (g + 1) * G, :] = f0[halo_k[g], g * G : (g + 1) * G, :]
    stage_traces(0, low)
    for i in range(2 * ROUNDS):
        res[i, 0:4] = jnp.zeros((4, FR, BV), BF16)
        res[i, 68:72] = jnp.zeros((4, FR, BV), BF16)

    pl.semaphore_wait(barrier, count)
    to_neighbours(0, halo_out, halo_out, lambda s: halo_f.at[0, s])
    to_neighbours(2, tl_out.at[0], tl_out.at[0], lambda s: tl_in.at[0, s])

    for r in range(ROUNDS):
        source = f0 if r == 0 else foot.at[0]
        def first_edges():
            if r == 0:
                from_neighbours(0, lambda s: halo_f.at[0, s])
                from_neighbours(2, lambda s: tl_in.at[0, s])
            else:
                for side in range(2):
                    from_frames(6 + side, r - 1, lambda at, side=side: halo_f.at[r, side, group_rows(at)])
            edges(2 * r, source, four(low), r, r, True)
            to_neighbours(5 + 2 * r, dr_out.at[r, 0], dr_out.at[r, 1], lambda s: dr_in.at[r, s])

        gram = gram_of(source)
        if r > 0:
            first_edges()
        inverse = inverse_blocks(fold_diagonal(gram), RIDGE_TRACE)
        weights = dot(gram, inverse, HIGH)

        if r == 0:
            loads[0].wait()
            loads[1].wait()
        middle(2 * r, source, four(low), r, 1, 7)
        if r == 0:
            first_edges()
        gather(2 * r)
        cross = jnp.zeros((NG * FR, NC), F32)
        for k in range(BPG):
            cross = cross + dot_nt(pieces[k], source[k])
        drives = jnp.zeros((FR, NC), F32)
        for g in range(NG):
            drives = drives + jnp.where(group32 == g, cross[g * FR : (g + 1) * FR], 0.0)
        from_neighbours(5 + 2 * r, lambda s: dr_in.at[r, s])
        drives = drives + (dr_in[r, 0] + dr_in[r, 1])
        drives = dot(drives, inverse, HIGH)
        high, rest = halves(weights)
        weights = jnp.concatenate([high, high, rest], axis=0)
        current = traces_now
        for p in range(NG):
            high, rest = halves(current - traces_now)
            coupled = dot(jnp.concatenate([high, rest, high], axis=1), weights)
            fresh = jnp.maximum(current + (drives - coupled), 0.0)
            current = jnp.where(group32 == bl[BPG, p], fresh, current)
        traces_now = current
        low = traces_now.astype(BF16)

        stage_traces(r + 1, low)
        to_neighbours(3 + r, tl_out.at[r + 1], tl_out.at[r + 1], lambda s: tl_in.at[r + 1, s])
        corr = lax.dot_general(
            traces_now, traces_now, (((0,), (0,)), ((), ())), precision=HIGH, preferred_element_type=F32
        )
        sq = [jnp.sum(bts[c] * bts[c], axis=0, keepdims=True) for c in range(2)]
        corr_out[r, 0:G, :] = fold_diagonal(corr)
        corr_out[r, G : G + 4, :] = jnp.broadcast_to(sq[0], (4, NC))
        corr_out[r, G + 4 : G + 8, :] = jnp.broadcast_to(sq[1], (4, NC))
        to_frames(0, r, lambda to: corr_out.at[r], lambda at: corr_in.at[r, at])

        inst = 2 * r + 1
        middle(inst, source, four(low), r, 1, 7)
        lane = lanes(FR)
        spread = jnp.zeros((FR, NC), F32)
        for c in range(2):
            for s, part in enumerate(split3(bts[c])):
                spread = jnp.where(lane // 8 == s * 2 + c, part, spread)
        stacked = jnp.concatenate(
            [jnp.where(lane % 8 == b, spread, 0.0).astype(BF16) for b in range(8)], axis=0
        )
        btm[...] = dot_nt(eye[0:48].astype(BF16), stacked).astype(BF16)
        vacc[...] = jnp.zeros_like(vacc)

        from_neighbours(3 + r, lambda s: tl_in.at[r + 1, s])
        edges(inst, source, four(low), r + 1, r, False)
        cat = 5 + inst
        to_neighbours(
            cat, res.at[inst, pl.ds(4, 4)], res.at[inst, pl.ds(64, 4)], lambda s: edge_in.at[r, pl.ds(4 * s, 4)]
        )

        from_frames(0, r, lambda at: corr_in.at[r, at])
        corr_in[r, me] = corr_out[r]
        total = corr_in[r, 0]
        for s in range(1, NT):
            total = total + corr_in[r, s]
        inverse_a = inverse_blocks(total[0:G], RIDGE_FOOT)
        square_time = [total[G : G + 1], total[G + 4 : G + 5]]
        masked = jnp.concatenate(
            [jnp.where(group32 == g, low.astype(F32), 0.0) for g in range(NG)], axis=0
        )
        z = dot_nt(inverse_a, masked, HIGH)
        z_high = z.astype(BF16)
        zs[0] = z_high
        zs[1] = (z - z_high.astype(F32)).astype(BF16)

        for g in range(NG):
            for k in range(BPG - 1):
                at = jnp.where(halo_k[g] <= k, entry[g][k + 1], entry[g][k])
                pieces[k, g * FR : (g + 1) * FR, :] = res[inst, at]
        for k in range(BPG - 1):
            part_out[r, k] = (dot(zs[0], pieces[k]) + dot(zs[1], pieces[k])).astype(BF16)
        to_frames(1, r, lambda to: part_out.at[r, :, group_rows(to)], lambda at: part_in.at[r, at])

        background(inst, r)
        to_frames(3, r, lambda to: frame_out.at[r, to], lambda at: frame_in.at[r, at])

        from_neighbours(cat, lambda s: edge_in.at[r, pl.ds(4 * s, 4)])
        for g in range(NG):
            block = edge_in[r, halo_at[g]]
            own = res[inst, jnp.where(halo_any[g], 4, entry[g][0])]
            edge_pieces[g * FR : (g + 1) * FR, :] = jnp.where(
                halo_any[g], block.astype(F32), own.astype(F32)
            ).astype(BF16)
        edge_out[r] = (dot(zs[0], edge_pieces[...]) + dot(zs[1], edge_pieces[...])).astype(BF16)
        to_frames(2, r, lambda to: edge_out.at[r, group_rows(to)], lambda at: edge_sum.at[r, at])

        row = lax.broadcasted_iota(jnp.int32, (FR, 48), 0)
        col = lax.broadcasted_iota(jnp.int32, (FR, 48), 1)
        summed = jnp.zeros((FR, 48), F32)
        for b in range(8):
            summed = summed + jnp.where(col % 8 == b, vacc[b * FR : (b + 1) * FR, :], 0.0)
        packed = jnp.zeros((FR, NC), F32)
        for c in range(2):
            total = jnp.sum(jnp.where((col // 8) % 2 == c, summed, 0.0), axis=1, keepdims=True)
            packed = jnp.where(lane == c, total, packed)
            squares = jnp.zeros((8, BV), F32)
            for j in range(8):
                part = field(r, j)[c * 8 : (c + 1) * 8]
                squares = squares + part * part
            squares = jnp.sum(jnp.sum(squares, axis=0, keepdims=True), axis=1, keepdims=True)
            packed = jnp.where(lane == 2 + c, squares, packed)

        def level_send(i, value):
            q, rows = peers[i]
            vox[r, i, q] = value
            for other, oq in rows:
                send(vox.at[r, i, q], vox.at[r, i, q], vx_s.at[r, i, oq], vx_r.at[r, i, q], (other, me))

        def level_sum(i):
            q, rows = peers[i]
            for other, oq in rows:
                arrived(vox.at[r, i, oq], vx_s.at[r, i, oq], vx_r.at[r, i, oq], (other, me))
            total = vox[r, i, 0]
            for s in range(1, levels[i][1]):
                total = total + vox[r, i, s]
            return total

        level_send(0, dot_nt(eye[0:8], packed, HIGH))

        frame = frame_out[r, me].astype(F32)
        from_frames(3, r, lambda at: frame_in.at[r, at])
        for d in range(1, NT):
            frame = frame + frame_in[r, lax.rem(me + d, NT)].astype(F32)
        scale = jnp.concatenate([jnp.broadcast_to(square_time[c], (8, NC)) for c in range(2)], axis=0)
        scale = jnp.concatenate([scale] * (BV // NC), axis=1)
        bgs[r, me] = jnp.maximum(field(r, me) + frame / (2.0 * scale), 0.0).astype(BF16)
        to_frames(5, r, lambda to: bgs.at[r, me], lambda at: bgs.at[r, at])
        my_rows = group_rows(me)
        total = part_out[r, :, my_rows].astype(F32)
        from_frames(1, r, lambda at: part_in.at[r, at])
        for d in range(1, NT):
            total = total + part_in[r, lax.rem(me + d, NT)].astype(F32)
        from_frames(2, r, lambda at: edge_sum.at[r, at])
        extra = edge_out[r, my_rows].astype(F32)
        for d in range(1, NT):
            extra = extra + edge_sum[r, lax.rem(me + d, NT)].astype(F32)
        which = jnp.int32(0)
        for k in range(BPG):
            mine = bl[k, me]
            which = jnp.where(jnp.logical_or(mine < 4, mine >= 68), k, which)
        for k in range(BPG):
            moved = jnp.where(which < k, total[max(k - 1, 0)], total[min(k, BPG - 2)])
            moved = jnp.where(which == k, extra, moved)
            fresh = jnp.maximum(source[k, my_rows, :].astype(F32) + moved, 0.0)
            foot[r, k, my_rows, :] = fresh.astype(BF16)
            spill = fresh if k == 0 else jnp.where(which == k, fresh, spill)
        last = r + 1 == ROUNDS
        if not last:
            halo_row[...] = spill.astype(BF16)
            to_neighbours(1, halo_row, halo_row, lambda s: halo_f.at[r + 1, s, my_rows])
        to_frames(4, r, lambda to: foot.at[r, :, my_rows], lambda at: foot.at[r, :, group_rows(at)])
        if not last:
            from_neighbours(1, lambda s: halo_f.at[r + 1, s, my_rows])
            for side in range(2):
                to_frames(
                    6 + side,
                    r,
                    lambda to, side=side: halo_f.at[r + 1, side, my_rows],
                    lambda at, side=side: halo_f.at[r + 1, side, group_rows(at)],
                )
        level_send(1, level_sum(0))
        from_frames(5, r, lambda at: bgs.at[r, at])
        from_frames(4, r, lambda at: foot.at[r, :, group_rows(at)])
        packed = level_sum(1)
        for c in range(2):
            change = packed[c : c + 1] / (2.0 * packed[2 + c : 3 + c])
            change = dot_nt(eye32, jnp.broadcast_to(change, (NC, FR)), HIGH)
            bts[c] = jnp.maximum(bts[c] + change, 0.0)

    out_tr[...] = dot_nt(eye, traces_now, HIGH)
    out_f[...] = foot[ROUNDS - 1]
    out_bg[...] = bgs[ROUNDS - 1]
    both = jnp.where(lanes(FR) == 0, bts[0], jnp.where(lanes(FR) == 1, bts[1], 0.0))
    out_bt[...] = dot_nt(eye[0:8], both, HIGH)[0:2]
    for copy in sends:
        copy.wait_send()


def solution(mesh):
    nsp = mesh.shape["space"]
    near = min(8, nsp)
    levels = ((1, near), (near, nsp // near))
    vmem = pl.BlockSpec(memory_space=pltpu.VMEM)
    far = pl.BlockSpec(memory_space=pltpu.HBM)
    smem = pl.BlockSpec(memory_space=pltpu.SMEM)

    def body(activity, footprints, traces, bg_space, bg_time, block_lists, group_order):
        f0 = footprints[0].reshape(NC, BPG, BV).transpose(1, 0, 2)
        small = jnp.concatenate([traces.reshape(NC, FR), bg_time], axis=0)
        lists = jnp.concatenate([block_lists[0].T, group_order], axis=0)
        out_tr, out_f, out_bg, out_bt = pl.pallas_call(
            functools.partial(kernel, nsp, levels),
            out_shape=(
                jax.ShapeDtypeStruct((NC, FR), F32),
                jax.ShapeDtypeStruct((BPG, NC, BV), BF16),
                jax.ShapeDtypeStruct((8, 16, BV), BF16),
                jax.ShapeDtypeStruct((2, FR), F32),
            ),
            in_specs=[far, vmem, vmem, far, smem],
            out_specs=(vmem,) * 4,
            scratch_shapes=[
                pltpu.VMEM((VB, FR, BV), BF16),
                pltpu.VMEM((2, VB, BV), F32),
                pltpu.VMEM((FR, BPG * NC), jnp.int32),
                pltpu.VMEM((2 * ROUNDS, EXT, FR, BV), BF16),
                pltpu.VMEM((BPG, NG * FR, BV), BF16),
                pltpu.VMEM((ROUNDS, BPG, NC, BV), BF16),
                pltpu.VMEM((ROUNDS, 8, 16, BV), BF16),
                pltpu.VMEM((2, FR, NC), F32),
                pltpu.VMEM((ROUNDS, 2, NC, BV), BF16),
                pltpu.VMEM((NC, BV), BF16),
                pltpu.VMEM((G, BV), BF16),
                pltpu.VMEM((ROUNDS + 1, 2, FR + G, NC), BF16),
                pltpu.VMEM((ROUNDS + 1, FR + G, NC), BF16),
                pltpu.VMEM((ROUNDS, 2, FR, NC), F32),
                pltpu.VMEM((ROUNDS, 2, FR, NC), F32),
                pltpu.VMEM((ROUNDS, G + 8, NC), F32),
                pltpu.VMEM((ROUNDS, NT, G + 8, NC), F32),
                pltpu.VMEM((ROUNDS, BPG - 1, NC, BV), BF16),
                pltpu.VMEM((ROUNDS, NT, BPG - 1, G, BV), BF16),
                pltpu.VMEM((ROUNDS, 8, FR, BV), BF16),
                pltpu.VMEM((NG * FR, BV), BF16),
                pltpu.VMEM((ROUNDS, NC, BV), BF16),
                pltpu.VMEM((ROUNDS, NT, G, BV), BF16),
                pltpu.VMEM((ROUNDS, NT, 16, BV), BF16),
                pltpu.VMEM((ROUNDS, NT, 16, BV), BF16),
                pltpu.VMEM((8 * FR, 48), F32),
                pltpu.VMEM((ROUNDS, 2, 8, 8, FR), F32),
                pltpu.VMEM((2, NC, NG * FR), BF16),
                pltpu.VMEM((48, 8 * FR), BF16),
                pltpu.SemaphoreType.DMA((2,)),
                pltpu.SemaphoreType.DMA((9, 2)),
                pltpu.SemaphoreType.DMA((9, 2)),
                pltpu.SemaphoreType.DMA((8, ROUNDS, NT)),
                pltpu.SemaphoreType.DMA((8, ROUNDS, NT)),
                pltpu.SemaphoreType.DMA((ROUNDS, 2, 8)),
                pltpu.SemaphoreType.DMA((ROUNDS, 2, 8)),
            ],
            compiler_params=pltpu.CompilerParams(
                collective_id=0, has_side_effects=True, vmem_limit_bytes=52 * 1024 * 1024
            ),
        )(activity, f0, small, bg_space, lists)
        return (
            out_tr.reshape(1, NG, G, FR),
            out_f.transpose(1, 0, 2).reshape(1, NG, G, BPG, BV),
            out_bg.reshape(8, 2, 8, BV).transpose(1, 0, 2, 3).reshape(2, VB, BV).astype(F32),
            out_bt,
        )

    return jax.shard_map(
        body,
        mesh=mesh,
        in_specs=(
            P("space", "tm", None),
            P("space", None, None, None, None),
            P("space", None, None, "tm"),
            P(None, "space", None),
            P(None, "tm"),
            P("space", None, None),
            P("space", None),
        ),
        out_specs=(
            P("space", None, None, "tm"),
            P("space", None, None, None, None),
            P(None, "space", None),
            P(None, "tm"),
        ),
        check_vma=False,
    )
```
